32 devices in a mesh: blk: 8 (over y, x, core), tp: 4 (over z).
Axes of the slice: x: 2, y: 2, z: 4, core: 2. Of those that a mesh axis runs over, the one named last changes fastest.
Arguments:
- tokens: bfloat16 [8192, 896], P(('blk', 'tp')), may hold values from -6 to 6
- cotangent: bfloat16 [8192, 896], P(('blk', 'tp')), may hold values from -0.59765625 to 0.59765625
- weights: bfloat16 [8, 608, 3, 896], P('blk', 'tp'), may hold values from -6 to 6
- first_moment: bfloat16 [8, 608, 3, 896], P('blk', 'tp'), may hold values from -0.1796875 to 0.1796875
- second_moment: bfloat16 [8, 608, 3, 896], P('blk', 'tp'), may hold values from 0.0009994507 to 0.0099487305
Outputs:
- averaged: float32 [8, 608, 3, 896], P('blk', 'tp')
The draws below stay inside these ranges and needn't reach their ends.
All inputs are finite; a program needn't handle non-finite values.
Results may differ from the reference program's by a relative error of at most 0.0003.
Values may be sent and summed in bfloat16 or wider, within the bound.
No kernel may reach another device: no remote copies, remote signals or barrier semaphores. Data moves between devices by JAX's collectives and lax.ppermute only.
A program may use at most 64 MiB of HBM per device.

```python
import math
import jax
import jax.numpy as jnp
from jax import lax

D = 896
TOK_DEV = 256
STEP = 10
FFW = 608
REPLICAS = 8
TOKENS = 8192
N_BLK = 8
N_TP = 4


def block_levels(stream_key, shape, cuts, low, largest):
    loudness = 1.0
    for position, blocks in cuts:
        draws = jax.random.uniform(jax.random.fold_in(jax.random.fold_in(stream_key, 6), position), (blocks,), jnp.float32, low / len(cuts), largest / len(cuts))
        loudness = loudness * jnp.repeat(jnp.exp(draws), shape[position] // blocks).reshape((-1,) + (1,) * (len(shape) - 1 - position))
    return loudness


def bell_draw(stream_key, extent, width, most, cuts=(), held_as=jnp.bfloat16):
    array = jax.random.normal(stream_key, extent, jnp.float32) * width
    if len(cuts) > 0:
        array = block_levels(stream_key, extent, cuts, -0.22, 0.18) * array
    return jnp.clip(array, min=-most, max=most).astype(held_as)


def setup_inputs(seed: int = 0) -> dict:
    key_of = jax.random.split(jax.random.key(seed), 6)
    tokens = bell_draw(key_of[0], (TOKENS, D), 1.0, 6.0, ((0, 32),))
    cotangent = bell_draw(key_of[1], (TOKENS, D), 0.1, 0.59765625, ((0, 32),))
    weights = bell_draw(key_of[2], (REPLICAS, FFW, 3, D), 1.0, 6.0, ((0, 8), (1, 4)))
    first_moment = bell_draw(key_of[3], (REPLICAS, FFW, 3, D), 0.03, 0.1796875, ((0, 8), (1, 4)))
    second_moment = jnp.clip(jnp.exp(math.log(0.0099487305) - 2.2979944 * jax.random.uniform(key_of[4], (REPLICAS, FFW, 3, D), jnp.float32) ** block_levels(key_of[4], (REPLICAS, FFW, 3, D), ((0, 8), (1, 4)), -0.2, 0.2)), 0.0009994507, 0.0099487305).astype(jnp.bfloat16)
    return dict(tokens=tokens, cotangent=cotangent, weights=weights, first_moment=first_moment, second_moment=second_moment)


def row_terms(xs, grads_out, rows):
    width_scale = D ** (-0.5)
    hidden_scale = FFW ** (-0.5)
    gate = jnp.dot(xs, rows[:, 0, :].T, preferred_element_type=jnp.float32) * width_scale
    upper = jnp.dot(xs, rows[:, 1, :].T, preferred_element_type=jnp.float32) * width_scale
    sigma = jax.nn.sigmoid(gate)
    swish = gate * sigma
    hidden = (swish * upper).astype(jnp.bfloat16)
    back = jnp.dot(grads_out, rows[:, 2, :].T, preferred_element_type=jnp.float32) * hidden_scale
    dgate = (back * upper * sigma * (1.0 + gate * (1.0 - sigma))).astype(jnp.bfloat16)
    dupper = (back * swish).astype(jnp.bfloat16)
    grad_gate = jnp.dot(dgate.T, xs, preferred_element_type=jnp.float32) * width_scale
    grad_upper = jnp.dot(dupper.T, xs, preferred_element_type=jnp.float32) * width_scale
    grad_down = jnp.dot(hidden.T, grads_out, preferred_element_type=jnp.float32) * hidden_scale
    return jnp.stack([grad_gate, grad_upper, grad_down], axis=1)

def reference(tokens, cotangent, weights, first_moment, second_moment):
    token_blocks = tokens.reshape(N_BLK, N_TP * TOK_DEV, D)
    cot_blocks = cotangent.reshape(N_BLK, N_TP * TOK_DEV, D)

    def replica(packed):
        return row_terms(packed[0], packed[1], packed[2])
    grads = lax.map(replica, (token_blocks, cot_blocks, weights))
    moment_one = 0.9 * first_moment.astype(jnp.float32) + 0.1 * grads
    moment_two = 0.95 * second_moment.astype(jnp.float32) + 0.05 * grads * grads
    correct_one = 1.0 - 0.9 ** STEP
    correct_two = 1.0 - 0.95 ** STEP
    master = weights.astype(jnp.float32)
    step_size = moment_one / correct_one / (jnp.sqrt(moment_two / correct_two) + 1e-08)
    updated = master - 0.1 * (step_size + 0.1 * master)
    return (jnp.roll(updated, 1, axis=0) + updated + jnp.roll(updated, -1, axis=0)) / 3.0
```

```python
import jax
import jax.numpy as jnp
from jax import lax
from jax.sharding import PartitionSpec as P

STEP = 10
CORRECT_ONE = 1.0 - 0.9**STEP
CORRECT_TWO = 1.0 - 0.95**STEP


def shifted(block, axis, distance):
    count = lax.axis_size(axis)
    return lax.ppermute(block, axis, [((i - distance) % count, i) for i in range(count)])


def adam_step(moment_one, moment_two):
    return moment_one / CORRECT_ONE / (jnp.sqrt(moment_two / CORRECT_TWO) + 1e-08)


def unit_grads(xs, cots, rows, hidden_scale):
    width_scale = xs.shape[1] ** (-0.5)

    def into_units(values, matrix):
        return jnp.einsum("td,nd->nt", values, matrix, preferred_element_type=jnp.float32)

    def over_tokens(terms, values):
        return jnp.einsum("nt,td->nd", terms, values, preferred_element_type=jnp.float32)

    gate = into_units(xs, rows[0]) * width_scale
    upper = into_units(xs, rows[1]) * width_scale
    sigma = jax.nn.sigmoid(gate)
    swish = gate * sigma
    hidden = (swish * upper).astype(jnp.bfloat16)
    back = into_units(cots, rows[2]) * hidden_scale
    dgate = (back * upper * sigma * (1.0 + gate * (1.0 - sigma))).astype(jnp.bfloat16)
    dupper = (back * swish).astype(jnp.bfloat16)
    return (
        over_tokens(dgate, xs) * width_scale,
        over_tokens(dupper, xs) * width_scale,
        over_tokens(hidden, cots) * hidden_scale,
    )


def line_of_four(tokens, cots, rows, hidden_scale):
    inward = [(0, 1), (3, 2)]
    middle = [(1, 2), (2, 1)]
    outward = [(1, 0), (2, 3)]
    units = rows.shape[1]

    def send(block, route):
        return lax.ppermute(block, "tp", route)

    outer_x = send(tokens, inward)
    inner_x = send(tokens, middle)
    outer_g = send(cots, inward)
    inner_g = send(cots, middle)
    far_x = send(outer_x, middle)
    far_g = send(outer_g, middle)
    outer_rows = send(rows, inward)
    both_rows = jnp.concatenate([rows, outer_rows], axis=1)
    near = unit_grads(
        jnp.concatenate([tokens, outer_x, inner_x]),
        jnp.concatenate([cots, outer_g, inner_g]),
        both_rows,
        hidden_scale,
    )
    far = unit_grads(far_x, far_g, both_rows, hidden_scale)
    place = lax.axis_index("tp")
    inside = (place == 1) | (place == 2)
    grads = []
    for k in (2, 1, 0):
        whole = near[k] + far[k]
        arrived = send(whole[units:].astype(jnp.bfloat16), outward)
        grads.append(jnp.where(inside, whole[:units], arrived.astype(jnp.float32)))
    return grads[::-1]


def gathered(tokens, cots, rows, hidden_scale):
    return unit_grads(
        lax.all_gather(tokens, "tp", axis=0, tiled=True),
        lax.all_gather(cots, "tp", axis=0, tiled=True),
        rows,
        hidden_scale,
    )


def on_device(tokens, cotangent, weights, first_moment, second_moment):
    rows = jnp.swapaxes(weights[0], 0, 1)
    hidden_scale = (rows.shape[1] * lax.axis_size("tp")) ** (-0.5)
    moment_one = 0.9 * jnp.swapaxes(first_moment[0], 0, 1).astype(jnp.float32)
    moment_two = 0.95 * jnp.swapaxes(second_moment[0], 0, 1).astype(jnp.float32)
    master = rows.astype(jnp.float32)
    still_step = adam_step(moment_one, moment_two)
    still = master - 0.1 * (still_step + 0.1 * master)
    still_sum = still + shifted(still, "blk", 1) + shifted(still, "blk", -1)
    plan = line_of_four if lax.axis_size("tp") == 4 else gathered
    grads = plan(tokens, cotangent, rows, hidden_scale)
    parts = [None] * 3
    for k in (2, 1, 0):
        step = adam_step(
            moment_one[k] + 0.1 * grads[k], moment_two[k] + 0.05 * grads[k] * grads[k]
        )
        change = 0.1 * (still_step[k] - step)
        sent = change.astype(jnp.bfloat16)
        around = shifted(sent, "blk", 1).astype(jnp.float32) + shifted(sent, "blk", -1).astype(
            jnp.float32
        )
        parts[k] = (still_sum[k] + change + around) / 3.0
    return jnp.swapaxes(jnp.stack(parts), 0, 1)[None]


def solution(mesh):
    in_specs = (
        P(("blk", "tp"), None),
        P(("blk", "tp"), None),
        P("blk", "tp", None, None),
        P("blk", "tp", None, None),
        P("blk", "tp", None, None),
    )
    out_specs = P("blk", "tp", None, None)
    return jax.shard_map(
        on_device, mesh=mesh, in_specs=in_specs, out_specs=out_specs, check_vma=False
    )
```

```python
import functools

import jax
import jax.numpy as jnp
from jax import lax
from jax.experimental import pallas as pl
from jax.experimental.pallas import tpu as pltpu
from jax.sharding import PartitionSpec as P

STEP = 10
CORRECT_ONE = 1.0 - 0.9**STEP
CORRECT_TWO = 1.0 - 0.95**STEP
HALF = jnp.bfloat16
FULL = jnp.float32
ORDER = (2, 1, 0)


def shifted(block, axis, distance):
    count = lax.axis_size(axis)
    return lax.ppermute(block, axis, [((i - distance) % count, i) for i in range(count)])


def adam_step(moment_one, moment_two):
    return moment_one / CORRECT_ONE / (jnp.sqrt(moment_two / CORRECT_TWO) + 1e-08)


def into_units(matrix, values):
    return lax.dot_general(matrix, values, (((1,), (1,)), ((), ())), preferred_element_type=FULL)


def over_tokens(terms, values):
    return lax.dot_general(terms, values, (((1,), (0,)), ((), ())), preferred_element_type=FULL)


def forward_terms(xs, gate_rows, upper_rows):
    scale = xs.shape[1] ** (-0.5)
    gate = into_units(gate_rows, xs) * scale
    upper = into_units(upper_rows, xs) * scale
    sigma = 1.0 / (1.0 + jnp.exp(-gate))
    swish = gate * sigma
    return (swish * upper).astype(HALF), swish, upper * sigma * (1.0 + gate * (1.0 - sigma))


def backward_terms(cots, down_rows, swish, slope, scale):
    back = into_units(down_rows, cots) * scale
    return (back * slope).astype(HALF), (back * swish).astype(HALF)


def unit_grads(xs, cots, rows, scale):
    hidden, swish, slope = forward_terms(xs, rows[0], rows[1])
    dgate, dupper = backward_terms(cots, rows[2], swish, slope, scale)
    width_scale = xs.shape[1] ** (-0.5)
    return jnp.stack(
        [
            over_tokens(dgate, xs) * width_scale,
            over_tokens(dupper, xs) * width_scale,
            over_tokens(hidden, cots) * scale,
        ]
    )


def call(kernel, outs, ins, after=(), flops=0, name=None):
    count = len(ins)

    def body(*refs):
        kernel(*refs[:count], *refs[count + len(after) :])

    return pl.pallas_call(
        body,
        out_shape=outs,
        in_specs=[pl.BlockSpec(memory_space=pltpu.VMEM)] * count
        + [pl.BlockSpec(memory_space=pl.ANY)] * len(after),
        out_specs=[pl.BlockSpec(memory_space=pltpu.VMEM)] * len(outs),
        cost_estimate=pl.CostEstimate(flops=flops, bytes_accessed=0, transcendentals=0),
        compiler_params=pltpu.CompilerParams(vmem_limit_bytes=32 * 2**20),
        name=name,
    )(*ins, *after)


def array(shape, dtype):
    return jax.ShapeDtypeStruct(shape, dtype)


def near_forward(own_x, pair_x, inner_x, rows, hidden, swish, slope):
    size = own_x.shape[0]
    for i, xs in enumerate((own_x, pair_x, inner_x)):
        place = pl.ds(i * size, size)
        hidden[:, place], swish[:, place], slope[:, place] = forward_terms(
            xs[...], rows[0], rows[1]
        )


def near_backward(
    own_x, pair_x, inner_x, own_g, pair_g, inner_g, rows, hidden, swish, slope, grads, *, scale
):
    size, width = own_x.shape
    totals = [0.0, 0.0, 0.0]
    for i, (xs, cots) in enumerate(((own_x, own_g), (pair_x, pair_g), (inner_x, inner_g))):
        place = pl.ds(i * size, size)
        dgate, dupper = backward_terms(
            cots[...], rows[2], swish[:, place], slope[:, place], scale
        )
        totals[0] += over_tokens(dgate, xs[...])
        totals[1] += over_tokens(dupper, xs[...])
        totals[2] += over_tokens(hidden[:, place], cots[...])
    for k in range(3):
        grads[k] = totals[k] * (scale if k == 2 else width ** (-0.5))


def ahead_forward(
    inner_x, far_x, inner_g, rows, pair_rows,
    far_hidden, far_swish, far_slope, hidden, swish, slope, dgate, dupper, *, scale
):
    size = inner_x.shape[0]
    first, second = pl.ds(0, size), pl.ds(size, size)
    hidden[:, first], near_swish, near_slope = forward_terms(
        inner_x[...], pair_rows[0], pair_rows[1]
    )
    dgate[...], dupper[...] = backward_terms(
        inner_g[...], pair_rows[2], near_swish, near_slope, scale
    )
    hidden[:, second], swish[...], slope[...] = forward_terms(
        far_x[...], pair_rows[0], pair_rows[1]
    )
    far_hidden[...], far_swish[...], far_slope[...] = forward_terms(far_x[...], rows[0], rows[1])


def pair_down(inner_g, far_g, hidden, sent, *, scale):
    size = inner_g.shape[0]
    total = over_tokens(hidden[:, :size], inner_g[...])
    total += over_tokens(hidden[:, size:], far_g[...])
    sent[...] = (total * scale).astype(HALF)


def pair_others(
    inner_x, far_x, far_g, pair_rows, swish, slope, dgate, dupper, sent_gate, sent_upper, *, scale
):
    width_scale = inner_x.shape[1] ** (-0.5)
    far_dgate, far_dupper = backward_terms(far_g[...], pair_rows[2], swish[...], slope[...], scale)
    total = over_tokens(dupper[...], inner_x[...]) + over_tokens(far_dupper, far_x[...])
    sent_upper[...] = (total * width_scale).astype(HALF)
    total = over_tokens(dgate[...], inner_x[...]) + over_tokens(far_dgate, far_x[...])
    sent_gate[...] = (total * width_scale).astype(HALF)


def far_backward(far_x, far_g, rows, hidden, swish, slope, near, grads, *, scale):
    width_scale = far_x.shape[1] ** (-0.5)
    dgate, dupper = backward_terms(far_g[...], rows[2], swish[...], slope[...], scale)
    grads[0] = near[0] + over_tokens(dgate, far_x[...]) * width_scale
    grads[1] = near[1] + over_tokens(dupper, far_x[...]) * width_scale
    grads[2] = near[2] + over_tokens(hidden[...], far_g[...]) * scale


def line_of_four(tokens, cots, rows, scale, still):
    pairs = [(0, 1), (1, 0), (2, 3), (3, 2)]
    middle = [(1, 2), (2, 1)]
    units, width = rows.shape[1:]
    size = tokens.shape[0]

    def send(block, route):
        return lax.ppermute(block, "tp", route)

    inner_x = send(tokens, middle)
    pair_x = send(tokens, pairs)
    inner_g = send(cots, middle)
    pair_g = send(cots, pairs)
    pair_rows = send(rows, pairs)
    far_x = send(pair_x, middle)
    far_g = send(pair_g, middle)
    work = 20_000_000_000
    near_terms = call(
        near_forward,
        [array((units, 3 * size), t) for t in (HALF, FULL, FULL)],
        (tokens, pair_x, inner_x, rows),
        after=(still,),
        flops=work,
        name="near_forward",
    )
    near = call(
        functools.partial(near_backward, scale=scale),
        [array((3, units, width), FULL)],
        (tokens, pair_x, inner_x, cots, pair_g, inner_g, rows, *near_terms),
        flops=work,
        name="near_backward",
    )[0]
    ahead = call(
        functools.partial(ahead_forward, scale=scale),
        [array((units, size), t) for t in (HALF, FULL, FULL)]
        + [array((units, 2 * size), HALF)]
        + [array((units, size), t) for t in (FULL, FULL, HALF, HALF)],
        (inner_x, far_x, inner_g, rows, pair_rows),
        after=(near,),
        name="ahead_forward",
    )
    far_terms, (hidden, swish, slope, dgate, dupper) = ahead[:3], ahead[3:]
    sent_down = call(
        functools.partial(pair_down, scale=scale),
        [array((units, width), HALF)],
        (inner_g, far_g, hidden),
        name="pair_down",
    )[0]
    sent_gate, sent_upper = call(
        functools.partial(pair_others, scale=scale),
        [array((units, width), HALF)] * 2,
        (inner_x, far_x, far_g, pair_rows, swish, slope, dgate, dupper),
        after=(sent_down,),
        name="pair_others",
    )
    grads = call(
        functools.partial(far_backward, scale=scale),
        [array((3, units, width), FULL)],
        (far_x, far_g, rows, *far_terms, near),
        after=(sent_gate,),
        name="far_backward",
    )[0]
    return grads, [send(v, pairs) for v in (sent_gate, sent_upper, sent_down)]


def gathered(tokens, cots, rows, scale):
    return unit_grads(
        lax.all_gather(tokens, "tp", axis=0, tiled=True),
        lax.all_gather(cots, "tp", axis=0, tiled=True),
        rows,
        scale,
    )


def still_kernel(rows, first, second, still):
    for k in range(3):
        master = rows[k].astype(FULL)
        step = adam_step(0.9 * first[k].astype(FULL), 0.95 * second[k].astype(FULL))
        still[k] = master - 0.1 * (step + 0.1 * master)


def base_kernel(still, before, after, base):
    base[...] = (still[...] + before[...] + after[...]) / 3.0


def change_kernel(grads, first, second, *rest, parts):
    *came, change, sent = rest
    grad = grads[0]
    for part in came[:parts]:
        grad = grad + part[...].astype(FULL)
    moment_one = 0.9 * first[0].astype(FULL)
    moment_two = 0.95 * second[0].astype(FULL)
    step = adam_step(moment_one + 0.1 * grad, moment_two + 0.05 * grad * grad)
    total = 0.1 * (adam_step(moment_one, moment_two) - step)
    change[...] = total
    sent[...] = total.astype(HALF)


def change_of(k, grads, first, second, came, after):
    units, width = grads.shape[1:]
    slab = pl.BlockSpec((1, units, width), lambda i: (k, 0, 0))
    whole = pl.BlockSpec((units, width), lambda i: (0, 0))
    return pl.pallas_call(
        functools.partial(change_kernel, parts=len(came)),
        grid=(1,),
        out_shape=[array((units, width), FULL), array((units, width), HALF)],
        in_specs=[slab] * 3 + [whole] * len(came) + [pl.BlockSpec(memory_space=pl.ANY)] * len(after),
        out_specs=[whole] * 2,
        cost_estimate=pl.CostEstimate(flops=0, bytes_accessed=0, transcendentals=0),
        compiler_params=pltpu.CompilerParams(vmem_limit_bytes=32 * 2**20),
        name=f"change_{k}",
    )(grads, first, second, *came, *after)


def finish_kernel(base, change, before, after, *rest):
    out = rest[-1]
    out[0] = base[0] + (change[...] + before[...].astype(FULL) + after[...].astype(FULL)) / 3.0


def finish(k, base, change, before, following, after):
    units, width = base.shape[1:]
    slab = pl.BlockSpec((1, units, width), lambda i: (k, 0, 0))
    whole = pl.BlockSpec((units, width), lambda i: (0, 0))
    return pl.pallas_call(
        finish_kernel,
        grid=(1,),
        out_shape=array(base.shape, FULL),
        in_specs=[slab] + [whole] * 3 + [pl.BlockSpec(memory_space=pl.ANY)] * len(after),
        out_specs=slab,
        input_output_aliases={0: 0},
        cost_estimate=pl.CostEstimate(flops=0, bytes_accessed=0, transcendentals=0),
        compiler_params=pltpu.CompilerParams(vmem_limit_bytes=32 * 2**20),
        name=f"finish_{k}",
    )(base, change, before, following, *after)


def on_device(tokens, cotangent, weights, first_moment, second_moment):
    rows, first, second = (
        jnp.swapaxes(v[0], 0, 1) for v in (weights, first_moment, second_moment)
    )
    slab = array(rows.shape, FULL)
    scale = (rows.shape[1] * lax.axis_size("tp")) ** (-0.5)
    still = call(still_kernel, [slab], (rows, first, second), name="still")[0]
    still_before, still_after = shifted(still, "blk", 1), shifted(still, "blk", -1)
    if lax.axis_size("tp") == 4:
        grads, came = line_of_four(tokens, cotangent, rows, scale, still)
        came = [[v] for v in came]
    else:
        grads, came = gathered(tokens, cotangent, rows, scale), [[]] * 3
    base = call(
        base_kernel, [slab], (still, still_before, still_after), after=(grads,), name="base"
    )[0]
    changes, last = [], (base,)
    for k in ORDER:
        change, sent = change_of(k, grads, first, second, came[k], last)
        changes.append((k, change, shifted(sent, "blk", 1), shifted(sent, "blk", -1)))
        last = (sent,)
    out = base
    for k, change, before, following in changes:
        out = finish(k, out, change, before, following, last)
        last = ()
    return jnp.swapaxes(out, 0, 1)[None]


def solution(mesh):
    in_specs = (
        P(("blk", "tp"), None),
        P(("blk", "tp"), None),
        P("blk", "tp", None, None),
        P("blk", "tp", None, None),
        P("blk", "tp", None, None),
    )
    out_specs = P("blk", "tp", None, None)
    return jax.shard_map(
        on_device, mesh=mesh, in_specs=in_specs, out_specs=out_specs, check_vma=False
    )
```

```python
import functools

import jax
import jax.numpy as jnp
from jax import lax
from jax.experimental import pallas as pl
from jax.experimental.pallas import tpu as pltpu
from jax.sharding import PartitionSpec as P

STEP = 10
CORRECT_ONE = 1.0 - 0.9**STEP
CORRECT_TWO = 1.0 - 0.95**STEP
HALF = jnp.bfloat16
FULL = jnp.float32
ORDER = (2, 1, 0)


def shifted(block, axis, distance):
    count = lax.axis_size(axis)
    return lax.ppermute(block, axis, [((i - distance) % count, i) for i in range(count)])


def adam_step(moment_one, moment_two):
    return moment_one / CORRECT_ONE / (jnp.sqrt(moment_two / CORRECT_TWO) + 1e-08)


def into_units(matrix, values):
    return lax.dot_general(matrix, values, (((1,), (1,)), ((), ())), preferred_element_type=FULL)


def over_tokens(terms, values):
    return lax.dot_general(terms, values, (((1,), (0,)), ((), ())), preferred_element_type=FULL)


def forward_terms(xs, gate_rows, upper_rows):
    scale = xs.shape[1] ** (-0.5)
    gate = into_units(gate_rows, xs) * scale
    upper = into_units(upper_rows, xs) * scale
    sigma = 1.0 / (1.0 + jnp.exp(-gate))
    swish = gate * sigma
    return (swish * upper).astype(HALF), swish, upper * sigma * (1.0 + gate * (1.0 - sigma))


def backward_terms(cots, down_rows, swish, slope, scale):
    back = into_units(down_rows, cots) * scale
    return (back * slope).astype(HALF), (back * swish).astype(HALF)


def unit_grads(xs, cots, rows, scale):
    hidden, swish, slope = forward_terms(xs, rows[0], rows[1])
    dgate, dupper = backward_terms(cots, rows[2], swish, slope, scale)
    width_scale = xs.shape[1] ** (-0.5)
    return jnp.stack(
        [
            over_tokens(dgate, xs) * width_scale,
            over_tokens(dupper, xs) * width_scale,
            over_tokens(hidden, cots) * scale,
        ]
    )


def call(kernel, outs, ins, after=(), flops=0, name=None):
    count = len(ins)

    def body(*refs):
        kernel(*refs[:count], *refs[count + len(after) :])

    return pl.pallas_call(
        body,
        out_shape=outs,
        in_specs=[pl.BlockSpec(memory_space=pltpu.VMEM)] * count
        + [pl.BlockSpec(memory_space=pl.ANY)] * len(after),
        out_specs=[pl.BlockSpec(memory_space=pltpu.VMEM)] * len(outs),
        cost_estimate=pl.CostEstimate(flops=flops, bytes_accessed=0, transcendentals=0),
        compiler_params=pltpu.CompilerParams(vmem_limit_bytes=32 * 2**20),
        name=name,
    )(*ins, *after)


def array(shape, dtype):
    return jax.ShapeDtypeStruct(shape, dtype)


def near_forward(own_x, pair_x, inner_x, rows, hidden, swish, slope):
    size = own_x.shape[0]
    for i, xs in enumerate((own_x, pair_x, inner_x)):
        place = pl.ds(i * size, size)
        hidden[:, place], swish[:, place], slope[:, place] = forward_terms(
            xs[...], rows[0], rows[1]
        )


def near_backward(
    own_x, pair_x, inner_x, own_g, pair_g, inner_g,
    rows, hidden, swish, slope, grads, *, scale
):
    size, width = own_x.shape
    totals = [0.0, 0.0, 0.0]
    shards = ((own_x, (own_g,)), (pair_x, (pair_g,)), (inner_x, (inner_g,)))
    for i, (xs, parts) in enumerate(shards):
        place = pl.ds(i * size, size)
        cots = joined(parts)
        dgate, dupper = backward_terms(cots, rows[2], swish[:, place], slope[:, place], scale)
        totals[0] += over_tokens(dgate, xs[...])
        totals[1] += over_tokens(dupper, xs[...])
        totals[2] += over_tokens(hidden[:, place], cots)
    for k in range(3):
        grads[k] = totals[k] * (scale if k == 2 else width ** (-0.5))


def ahead_forward(
    inner_x, far_x, inner_g, rows, pair_rows,
    far_hidden, far_swish, far_slope, hidden, swish, slope, dgate, dupper, *, scale
):
    size = inner_x.shape[0]
    first, second = pl.ds(0, size), pl.ds(size, size)
    hidden[:, first], near_swish, near_slope = forward_terms(
        inner_x[...], pair_rows[0], pair_rows[1]
    )
    dgate[...], dupper[...] = backward_terms(
        inner_g[...], pair_rows[2], near_swish, near_slope, scale
    )
    hidden[:, second], swish[...], slope[...] = forward_terms(
        far_x[...], pair_rows[0], pair_rows[1]
    )
    far_hidden[...], far_swish[...], far_slope[...] = forward_terms(far_x[...], rows[0], rows[1])


def pair_down(inner_g, far_g, hidden, sent, *, start, scale):
    size = inner_g.shape[0]
    columns = pl.ds(start, far_g.shape[1])
    total = over_tokens(hidden[:, :size], inner_g[:, columns])
    total += over_tokens(hidden[:, size:], far_g[...])
    sent[...] = (total * scale).astype(HALF)


def joined(parts):
    return jnp.concatenate([v[...] for v in parts], axis=1)


def pair_upper(
    inner_x, far_x, far_g, pair_rows, swish, slope, dgate, dupper, sent, far_dgate, *, scale
):
    width_scale = inner_x.shape[1] ** (-0.5)
    far_dgate[...], far_dupper = backward_terms(
        far_g[...], pair_rows[2], swish[...], slope[...], scale
    )
    total = over_tokens(dupper[...], inner_x[...]) + over_tokens(far_dupper, far_x[...])
    sent[...] = (total * width_scale).astype(HALF)


def pair_gate(inner_x, far_x, dgate, far_dgate, sent):
    width_scale = inner_x.shape[1] ** (-0.5)
    total = over_tokens(dgate[...], inner_x[...]) + over_tokens(far_dgate[...], far_x[...])
    sent[...] = (total * width_scale).astype(HALF)


def far_backward(far_x, far_g, rows, hidden, swish, slope, near, grads, *, scale):
    width_scale = far_x.shape[1] ** (-0.5)
    cots = far_g[...]
    dgate, dupper = backward_terms(cots, rows[2], swish[...], slope[...], scale)
    grads[0] = near[0] + over_tokens(dgate, far_x[...]) * width_scale
    grads[1] = near[1] + over_tokens(dupper, far_x[...]) * width_scale
    grads[2] = near[2] + over_tokens(hidden[...], cots) * scale


def line_of_four(tokens, cots, rows, sent_rows, scale):
    pairs = [(0, 1), (1, 0), (2, 3), (3, 2)]
    middle = [(1, 2), (2, 1)]
    units, width = rows.shape[1:]
    size = tokens.shape[0]

    def send(block, route):
        return lax.ppermute(block, "tp", route)

    inner_x = send(tokens, middle)
    pair_x = send(tokens, pairs)
    inner_g = send(cots, middle)
    pair_gs = [send(cots, pairs)]
    pair_rows = send(sent_rows, pairs)
    far_x = send(pair_x, middle)
    far_gs = [send(v, middle) for v in pair_gs]
    work = 20_000_000_000
    near_terms = call(
        near_forward,
        [array((units, 3 * size), t) for t in (HALF, FULL, FULL)],
        (tokens, pair_x, inner_x, rows),
        flops=work,
        name="near_forward",
    )
    near = call(
        functools.partial(near_backward, scale=scale),
        [array((3, units, width), FULL)],
        (tokens, pair_x, inner_x, cots, *pair_gs, inner_g, rows, *near_terms),
        name="near_backward",
    )[0]
    ahead = call(
        functools.partial(ahead_forward, scale=scale),
        [array((units, size), t) for t in (HALF, FULL, FULL)]
        + [array((units, 2 * size), HALF)]
        + [array((units, size), t) for t in (FULL, FULL, HALF, HALF)],
        (inner_x, far_x, inner_g, rows, pair_rows),
        after=(near,),
        flops=work,
        name="ahead_forward",
    )
    far_terms, (hidden, swish, slope, dgate, dupper) = ahead[:3], ahead[3:]
    pieces, last, start = [], (), 0
    for far_g in far_gs:
        sent = call(
            functools.partial(pair_down, start=start, scale=scale),
            [array((units, far_g.shape[1]), HALF)],
            (inner_g, far_g, hidden),
            after=last,
            name="pair_down",
        )[0]
        pieces.append(((2, start, far_g.shape[1]), [send(sent, pairs)]))
        last = (sent,)
        start += far_g.shape[1]
    sent, far_dgate = call(
        functools.partial(pair_upper, scale=scale),
        [array((units, width), HALF), array((units, size), HALF)],
        (inner_x, far_x, *far_gs, pair_rows, swish, slope, dgate, dupper),
        after=last,
        name="pair_upper",
    )
    pieces.append(((1, 0, width), [send(sent, pairs)]))
    sent = call(
        pair_gate,
        [array((units, width), HALF)],
        (inner_x, far_x, dgate, far_dgate),
        name="pair_gate",
    )[0]
    pieces.append(((0, 0, width), [send(sent, pairs)]))
    grads = call(
        functools.partial(far_backward, scale=scale),
        [array((3, units, width), FULL)],
        (far_x, *far_gs, rows, *far_terms, near),
        after=(sent,),
        name="far_backward",
    )[0]
    return grads, pieces


def gathered(tokens, cots, rows, scale):
    return unit_grads(
        lax.all_gather(tokens, "tp", axis=0, tiled=True),
        lax.all_gather(cots, "tp", axis=0, tiled=True),
        rows,
        scale,
    )


def still_kernel(rows, first, second, still, step, same_rows):
    master = rows[...].astype(FULL)
    total = adam_step(0.9 * first[...].astype(FULL), 0.95 * second[...].astype(FULL))
    step[...] = total
    still[...] = master - 0.1 * (total + 0.1 * master)
    same_rows[...] = rows[...]


def still_values(rows, first, second):
    units, width = rows.shape[1:]
    slab = pl.BlockSpec((1, units, width), lambda k: (k, 0, 0))
    return pl.pallas_call(
        still_kernel,
        grid=(3,),
        out_shape=[array(rows.shape, t) for t in (FULL, FULL, HALF)],
        in_specs=[slab] * 3,
        out_specs=[slab] * 3,
        compiler_params=pltpu.CompilerParams(vmem_limit_bytes=32 * 2**20),
        name="still",
    )(rows, first, second)


def base_kernel(still, before, after, base):
    base[...] = (still[...] + before[...] + after[...]) / 3.0


def change_kernel(grads, still_step, first, second, *rest, piece, parts):
    *came, change, sent = rest
    k, start, size = piece
    place = pl.ds(start, size)
    grad = grads[k, :, place]
    for part in came[:parts]:
        grad = grad + part[...].astype(FULL)
    moment_one = 0.9 * first[k, :, place].astype(FULL) + 0.1 * grad
    moment_two = 0.95 * second[k, :, place].astype(FULL) + 0.05 * grad * grad
    total = 0.1 * (still_step[k, :, place] - adam_step(moment_one, moment_two))
    change[...] = total
    sent[...] = total.astype(HALF)


def change_of(piece, grads, still_step, first, second, came, after):
    shape = (grads.shape[1], piece[2])
    return call(
        functools.partial(change_kernel, piece=piece, parts=len(came)),
        [array(shape, FULL), array(shape, HALF)],
        (grads, still_step, first, second, *came),
        after=after,
        name="change",
    )


def finish_kernel(base, change, before, following, *rest, piece, bands):
    out, total, done = rest[-3:]
    units = base.shape[1]
    k, start, size = piece
    columns = pl.ds(start, size)
    copies = []
    for i, band in enumerate(bands):
        place = pl.ds(band, (*bands, units)[i + 1] - band)
        around = before[place, :].astype(FULL) + following[place, :].astype(FULL)
        total[place, :] = base[k, place, columns] + (change[place, :] + around) / 3.0
        copies.append(
            pltpu.make_async_copy(total.at[place, :], out.at[k, place, columns], done.at[i])
        )
        copies[-1].start()
    for copy in copies:
        copy.wait()


def finish(piece, out, base, change, before, following, after):
    units = base.shape[1]
    bands = tuple(range(0, units - 15, 48))
    vmem, anywhere = pl.BlockSpec(memory_space=pltpu.VMEM), pl.BlockSpec(memory_space=pl.ANY)
    held = () if out is None else (out,)
    return pl.pallas_call(
        functools.partial(finish_kernel, piece=piece, bands=bands),
        out_shape=array(base.shape, FULL),
        in_specs=[vmem] * 4 + [anywhere] * (len(held) + len(after)),
        out_specs=anywhere,
        scratch_shapes=[
            pltpu.VMEM((units, piece[2]), FULL),
            pltpu.SemaphoreType.DMA((len(bands),)),
        ],
        input_output_aliases={4: 0} if held else {},
        cost_estimate=pl.CostEstimate(flops=2_000_000_000, bytes_accessed=0, transcendentals=0),
        compiler_params=pltpu.CompilerParams(vmem_limit_bytes=32 * 2**20),
        name="finish",
    )(base, change, before, following, *held, *after)


def on_device(tokens, cotangent, weights, first_moment, second_moment):
    rows, first, second = (
        jnp.swapaxes(v[0], 0, 1) for v in (weights, first_moment, second_moment)
    )
    scale = (rows.shape[1] * lax.axis_size("tp")) ** (-0.5)
    still, still_step, sent_rows = still_values(rows, first, second)
    still_before, still_after = shifted(still, "blk", 1), shifted(still, "blk", -1)
    if lax.axis_size("tp") == 4:
        grads, pieces = line_of_four(tokens, cotangent, rows, sent_rows, scale)
    else:
        grads = gathered(tokens, cotangent, rows, scale)
        pieces = [((k, 0, rows.shape[2]), []) for k in ORDER]
    base = call(
        base_kernel, [array(rows.shape, FULL)], (still, still_before, still_after), name="base"
    )[0]
    changes, last = [], (base,)
    for piece, came in pieces:
        change, sent = change_of(piece, grads, still_step, first, second, came, last)
        changes.append((piece, change, shifted(sent, "blk", 1), shifted(sent, "blk", -1)))
        last = (sent,)
    out = None
    for piece, change, before, following in changes:
        out = finish(piece, out, base, change, before, following, last)
        last = ()
    return jnp.swapaxes(out, 0, 1)[None]


def solution(mesh):
    in_specs = (
        P(("blk", "tp"), None),
        P(("blk", "tp"), None),
        P("blk", "tp", None, None),
        P("blk", "tp", None, None),
        P("blk", "tp", None, None),
    )
    out_specs = P("blk", "tp", None, None)
    return jax.shard_map(
        on_device, mesh=mesh, in_specs=in_specs, out_specs=out_specs, check_vma=False
    )
```

```python
import functools

import jax
import jax.numpy as jnp
from jax import lax
from jax.experimental import pallas as pl
from jax.experimental.pallas import tpu as pltpu
from jax.sharding import PartitionSpec as P

STEP = 10
CORRECT_ONE = 1.0 - 0.9**STEP
CORRECT_TWO = 1.0 - 0.95**STEP
HALF = jnp.bfloat16
FULL = jnp.float32
ORDER = (2, 1, 0)
AHEAD = 2
STILL_BY = 0
PIECES = (5, 6, 6)
NEAR_WORK = 5_000_000_000
PAIR_WORK = 20_000_000_000
AHEAD_WORK = 20_000_000_000
ACROSS_WORK = (20_000_000_000, 2_000_000_000, 2_000_000_000, 30_000_000_000)
FAR_WORK = 20_000_000_000


def neighbour(block, side):
    count = lax.axis_size("blk")
    if count % 2:
        route = [((i + 1 - 2 * side) % count, i) for i in range(count)]
    else:
        route = [((side + i) % count, (side + i + 1) % count) for i in range(0, count, 2)]
        route += [(j, i) for i, j in route]
    return lax.ppermute(block, "blk", route)


def adam_step(moment_one, moment_two):
    return moment_one / CORRECT_ONE / (jnp.sqrt(moment_two / CORRECT_TWO) + 1e-08)


def into_units(matrix, values):
    return lax.dot_general(matrix, values, (((1,), (1,)), ((), ())), preferred_element_type=FULL)


def over_tokens(terms, values):
    return lax.dot_general(terms, values, (((1,), (0,)), ((), ())), preferred_element_type=FULL)


def forward_terms(xs, gate_rows, upper_rows):
    scale = xs.shape[1] ** (-0.5)
    gate = into_units(gate_rows, xs) * scale
    upper = into_units(upper_rows, xs) * scale
    sigma = 1.0 / (1.0 + jnp.exp(-gate))
    swish = gate * sigma
    return (swish * upper).astype(HALF), swish, upper * sigma * (1.0 + gate * (1.0 - sigma))


def backward_terms(cots, down_rows, swish, slope, scale):
    back = into_units(down_rows, cots) * scale
    return (back * slope).astype(HALF), (back * swish).astype(HALF)


def unit_grads(xs, cots, rows, scale):
    hidden, swish, slope = forward_terms(xs, rows[0], rows[1])
    dgate, dupper = backward_terms(cots, rows[2], swish, slope, scale)
    width_scale = xs.shape[1] ** (-0.5)
    return jnp.stack(
        [
            over_tokens(dgate, xs) * width_scale,
            over_tokens(dupper, xs) * width_scale,
            over_tokens(hidden, cots) * scale,
        ]
    )


def call(kernel, outs, ins, after=(), flops=0, name=None):
    count = len(ins)

    def body(*refs):
        kernel(*refs[:count], *refs[count + len(after) :])

    return pl.pallas_call(
        body,
        out_shape=outs,
        in_specs=[pl.BlockSpec(memory_space=pltpu.VMEM)] * count
        + [pl.BlockSpec(memory_space=pl.ANY)] * len(after),
        out_specs=[pl.BlockSpec(memory_space=pltpu.VMEM)] * len(outs),
        cost_estimate=pl.CostEstimate(flops=flops, bytes_accessed=0, transcendentals=0),
        compiler_params=pltpu.CompilerParams(vmem_limit_bytes=32 * 2**20),
        name=name,
    )(*ins, *after)


def array(shape, dtype):
    return jax.ShapeDtypeStruct(shape, dtype)


def near_forward(*refs):
    *shards, rows, hidden, swish, slope = refs
    size = shards[0].shape[0]
    for i, xs in enumerate(shards):
        place = pl.ds(i * size, size)
        hidden[:, place], swish[:, place], slope[:, place] = forward_terms(
            xs[...], rows[0], rows[1]
        )


def joined(*parts):
    return jnp.concatenate([v[...] for v in parts], axis=1)


def inner_forward(*refs):
    near_forward(*refs[:-1])
    rows, top = refs[2], refs[-1]
    top[...] = rows[:2]


def near_backward(
    own_x, inner_x, pair_x, own_g, inner_g, pair_g,
    rows, hidden, swish, slope, pair_hidden, pair_swish, pair_slope, grads, more, *, scale
):
    size, width = own_x.shape
    more[...] = pair_g[:, width - more.shape[1] :]
    totals = [0.0, 0.0, 0.0]
    first, second = pl.ds(0, size), pl.ds(size, size)
    shards = (
        (own_x, own_g[...], hidden[:, first], swish[:, first], slope[:, first]),
        (inner_x, inner_g[...], hidden[:, second], swish[:, second], slope[:, second]),
        (pair_x, pair_g[...], pair_hidden[...], pair_swish[...], pair_slope[...]),
    )
    for xs, cots, hid, swi, slo in shards:
        dgate, dupper = backward_terms(cots, rows[2], swi, slo, scale)
        totals[0] += over_tokens(dgate, xs[...])
        totals[1] += over_tokens(dupper, xs[...])
        totals[2] += over_tokens(hid, cots)
    for k in range(3):
        grads[k] = totals[k] * (scale if k == 2 else width ** (-0.5))


def ahead_forward(inner_x, far_x, rows, pair_top, *terms):
    far_hidden, far_swish, far_slope, hidden, swish, slope = terms
    size = inner_x.shape[0]
    for i, xs in enumerate((inner_x, far_x)):
        place = pl.ds(i * size, size)
        hidden[:, place], swish[:, place], slope[:, place] = forward_terms(
            xs[...], pair_top[0], pair_top[1]
        )
    far_hidden[...], far_swish[...], far_slope[...] = forward_terms(far_x[...], rows[0], rows[1])


def ahead_backward(inner_g, pair_low, swish, slope, dgate, dupper, *, scale):
    size = inner_g.shape[0]
    dgate[...], dupper[...] = backward_terms(
        inner_g[...], pair_low[...], swish[:, :size], slope[:, :size], scale
    )


def pair_first(inner_x, inner_g, far_g, hidden, sent, *, scale):
    size = inner_x.shape[0]
    cut = sent.shape[1]
    total = over_tokens(hidden[:, :size], inner_g[:, :cut])
    total += over_tokens(hidden[:, size:], far_g[...])
    sent[...] = (total * scale).astype(HALF)


def pair_rest(
    inner_x, far_x, inner_g, far_g, more_g, pair_low, hidden, swish, slope, dgate, dupper,
    second, third, last, *, cut, scale
):
    size, width = inner_x.shape
    width_scale = width ** (-0.5)
    total = over_tokens(hidden[:, :size], inner_g[:, cut:])
    total += over_tokens(hidden[:, size:], more_g[...])
    columns = [(total * scale).astype(HALF)]
    far_terms = backward_terms(
        joined(far_g, more_g), pair_low[...], swish[:, size:], slope[:, size:], scale
    )
    for near, far in zip((dupper, dgate), far_terms[::-1]):
        total = over_tokens(near[...], inner_x[...]) + over_tokens(far, far_x[...])
        columns.append((total * width_scale).astype(HALF))
    columns = jnp.concatenate(columns, axis=1)
    start = 0
    for part in (second, third, last):
        part[...] = columns[:, start : start + part.shape[1]]
        start += part.shape[1]


def far_backward(far_x, far_g, more_g, rows, hidden, swish, slope, near, grads, *, scale):
    width_scale = far_x.shape[1] ** (-0.5)
    cots = joined(far_g, more_g)
    dgate, dupper = backward_terms(cots, rows[2], swish[...], slope[...], scale)
    grads[0] = near[0] + over_tokens(dgate, far_x[...]) * width_scale
    grads[1] = near[1] + over_tokens(dupper, far_x[...]) * width_scale
    grads[2] = near[2] + over_tokens(hidden[...], cots) * scale


def cut_columns(whole, rows, part, low):
    part[...] = whole[:, : part.shape[1]]
    low[...] = rows[2]


def line_of_four(tokens, cots, sent_cots, cuts, rows, still, scale):
    pairs = [(0, 1), (1, 0), (2, 3), (3, 2)]
    middle = [(1, 2), (2, 1)]
    units, width = rows.shape[1:]
    size = tokens.shape[0]

    def send(block, route):
        return lax.ppermute(block, "tp", route)

    inner_x = send(tokens, middle)
    pair_x = send(tokens, pairs)
    inner_g = send(cots, middle)
    pair_g = send(sent_cots, pairs)
    far_x = send(pair_x, middle)
    *near_terms, top = call(
        inner_forward,
        [array((units, 2 * size), t) for t in (HALF, FULL, FULL)]
        + [array((2, units, width), HALF)],
        (tokens, inner_x, rows),
        after=(still,),
        flops=NEAR_WORK,
        name="near_forward",
    )
    pair_top = send(top, pairs)
    pair_terms = call(
        near_forward,
        [array((units, size), t) for t in (HALF, FULL, FULL)],
        (pair_x, rows),
        after=near_terms[:1],
        flops=PAIR_WORK,
        name="pair_forward",
    )
    pair_part, low = call(
        cut_columns,
        [array((size, cuts[0]), HALF), array((units, width), HALF)],
        (pair_g, rows),
        after=pair_terms[:1],
        name="cut",
    )
    pair_low = send(low, pairs)
    near, pair_more = call(
        functools.partial(near_backward, scale=scale),
        [array((3, units, width), FULL), array((size, cuts[1]), HALF)],
        (tokens, inner_x, pair_x, cots, inner_g, pair_g, rows, *near_terms, *pair_terms),
        after=(pair_part,),
        name="near_backward",
    )
    far_gs = [send(v, middle) for v in (pair_part, pair_more)]
    ahead = call(
        ahead_forward,
        [array((units, size), t) for t in (HALF, FULL, FULL)]
        + [array((units, 2 * size), t) for t in (HALF, FULL, FULL)],
        (inner_x, far_x, rows, pair_top),
        after=(near,),
        flops=AHEAD_WORK,
        name="ahead_forward",
    )
    far_terms, (hidden, swish, slope) = ahead[:3], ahead[3:]
    sizes = [width * v // (7 * 128) * 128 for v in PIECES]
    sizes.append(3 * width - sum(sizes))
    cut, more = sizes[0], sizes[0] + sizes[1] - width
    ends = width - sizes[3]
    first = call(
        functools.partial(pair_first, scale=scale),
        [array((units, sizes[0]), HALF)],
        (inner_x, inner_g, far_gs[0], hidden),
        name="pair_first",
    )[0]
    dgate, dupper = call(
        functools.partial(ahead_backward, scale=scale),
        [array((units, size), HALF)] * 2,
        (inner_g, pair_low, swish, slope),
        after=(first,),
        name="ahead_backward",
    )
    grads = call(
        functools.partial(far_backward, scale=scale),
        [array((3, units, width), FULL)],
        (far_x, *far_gs, rows, *far_terms, near),
        after=(dgate,),
        flops=FAR_WORK,
        name="far_backward",
    )[0]
    second, third, last = call(
        functools.partial(pair_rest, cut=cut, scale=scale),
        [array((units, v), HALF) for v in sizes[1:]],
        (inner_x, far_x, inner_g, *far_gs, pair_low, hidden, swish, slope, dgate, dupper),
        after=(grads,),
        name="pair_rest",
    )
    pieces = [
        ([(2, 0, cut)], first),
        ([(2, cut, width - cut), (1, 0, more)], second),
        ([(1, more, width - more), (0, 0, ends)], third),
        ([(0, ends, sizes[3])], last),
    ]
    pieces = [(tuple(v for v in piece if v[2]), parts) for piece, parts in pieces]
    return grads, pieces, lambda block: send(block, pairs)


def gathered(tokens, cots, rows, scale):
    return unit_grads(
        lax.all_gather(tokens, "tp", axis=0, tiled=True),
        lax.all_gather(cots, "tp", axis=0, tiled=True),
        rows,
        scale,
    )


def still_kernel(rows, first, second, cots, still, step, same_cots):
    master = rows[...].astype(FULL)
    total = adam_step(0.9 * first[...].astype(FULL), 0.95 * second[...].astype(FULL))
    step[...] = total
    still[...] = master - 0.1 * (total + 0.1 * master)

    @pl.when(pl.program_id(0) == 0)
    def _():
        same_cots[...] = cots[...]


def still_values(rows, first, second, cots):
    slab = pl.BlockSpec((1, *rows.shape[1:]), lambda k: (k, 0, 0))
    whole = pl.BlockSpec(cots.shape, lambda k: (0, 0))
    return pl.pallas_call(
        still_kernel,
        grid=(3,),
        out_shape=[array(rows.shape, FULL)] * 2 + [array(cots.shape, cots.dtype)],
        in_specs=[slab] * 3 + [whole],
        out_specs=[slab] * 2 + [whole],
        compiler_params=pltpu.CompilerParams(vmem_limit_bytes=32 * 2**20),
        name="still",
    )(rows, first, second, cots)


def spans(piece):
    start = 0
    for k, first, size in piece:
        yield k, pl.ds(first, size), pl.ds(start, size)
        start += size


def columns_of(piece):
    return sum(size for _, _, size in piece)


def change_kernel(grads, still, still_step, first, second, *rest, piece, parts, ready):
    came, rest = rest[:parts], rest[parts:]
    ready, (updated, sent, *passed) = rest[:ready], rest[ready:]
    for block, same in zip(ready, passed):
        same[...] = block[...]
    for k, place, here in spans(piece):
        grad = grads[k, :, place]
        for part in came:
            grad = grad + part[:, here].astype(FULL)
        moment_one = 0.9 * first[k, :, place].astype(FULL) + 0.1 * grad
        moment_two = 0.95 * second[k, :, place].astype(FULL) + 0.05 * grad * grad
        total = 0.1 * (still_step[k, :, place] - adam_step(moment_one, moment_two))
        updated[:, here] = still[k, :, place] + total
        sent[:, here] = total.astype(HALF)


def change_of(piece, grads, still, still_step, first, second, came, ready, after):
    shape = (grads.shape[1], columns_of(piece))
    return call(
        functools.partial(change_kernel, piece=piece, parts=len(came), ready=len(ready)),
        [array(shape, FULL), array(shape, HALF)] + [array(v.shape, v.dtype) for v in ready],
        (grads, still, still_step, first, second, *came, *ready),
        after=after,
        name="change",
    )


def join_kernel(*refs):
    *blocks, joint = refs
    start = 0
    for block in blocks:
        joint[:, pl.ds(start, block.shape[1])] = block[...]
        start += block.shape[1]


def across_kernel(updated, still, far, total, *, piece):
    for k, place, here in spans(piece):
        total[:, here] = updated[:, here] + still[k, :, place] + far[:, here].astype(FULL)


def finish_kernel(*refs, pieces, bands):
    *parts, near, out, total, done = refs
    units = near.shape[0]
    copies, start = [], 0
    for part, piece in zip(parts, pieces):
        for k, place, here in spans(piece):
            there = pl.ds(start, place.size)
            for i, band in enumerate(bands):
                rows = pl.ds(band, (*bands, units)[i + 1] - band)
                total[rows, there] = (part[rows, here] + near[rows, there]) / 3.0
                copies.append(
                    pltpu.make_async_copy(
                        total.at[rows, there], out.at[k, rows, place], done.at[len(copies)]
                    )
                )
                copies[-1].start()
            start += place.size
    for copy in copies:
        copy.wait()


def finish(pieces, parts, near, shape):
    units = shape[1]
    bands = (0, units // 32 * 16)
    vmem = pl.BlockSpec(memory_space=pltpu.VMEM)
    return pl.pallas_call(
        functools.partial(finish_kernel, pieces=pieces, bands=bands),
        out_shape=array(shape, FULL),
        in_specs=[vmem] * (len(parts) + 1),
        out_specs=pl.BlockSpec(memory_space=pl.ANY),
        scratch_shapes=[
            pltpu.VMEM(near.shape, FULL),
            pltpu.SemaphoreType.DMA((2 * sum(len(v) for v in pieces),)),
        ],
        cost_estimate=pl.CostEstimate(flops=0, bytes_accessed=0, transcendentals=0),
        compiler_params=pltpu.CompilerParams(vmem_limit_bytes=32 * 2**20),
        name="finish",
    )(*parts, near)


def on_device(tokens, cotangent, weights, first_moment, second_moment):
    rows, first, second = (
        jnp.swapaxes(v[0], 0, 1) for v in (weights, first_moment, second_moment)
    )
    scale = (rows.shape[1] * lax.axis_size("tp")) ** (-0.5)
    width = rows.shape[2]
    cuts = (width * PIECES[0] // (7 * 128) * 128,)
    cuts += (width - cuts[0],)
    still, still_step, sent_cots = still_values(rows, first, second, cotangent)
    still_far = neighbour(still, 1)
    if lax.axis_size("tp") == 4:
        grads, pieces, send = line_of_four(
            tokens, cotangent, sent_cots, cuts, rows, still, scale
        )
    else:
        grads = gathered(tokens, cotangent, rows, scale)
        pieces = [([(k, 0, rows.shape[2])], None) for k in ORDER]
    came = [[] if v is None else [send(v)] for _, v in pieces[:AHEAD]]
    changes, last = [], ()
    for i, (piece, _) in enumerate(pieces):
        ready = [v for _, v in pieces[i + AHEAD : i + AHEAD + 1] if v is not None]
        updated, sent, *ready = change_of(
            piece, grads, still, still_step, first, second, came[i], ready, last
        )
        came.append([send(v) for v in ready])
        changes.append((piece, updated, neighbour(sent, 1)))
        last = (sent, still_far) if i == STILL_BY else (sent,)
    updates = [v for _, v, _ in changes]
    joint = call(
        join_kernel, [array((rows.shape[1], 3 * width), FULL)], updates, name="join"
    )[0]
    near = neighbour(joint, 0)
    totals, last = [], (joint,)
    for i, (piece, updated, far) in enumerate(changes):
        totals += call(
            functools.partial(across_kernel, piece=piece),
            [array(updated.shape, FULL)],
            (updated, still_far, far),
            after=last,
            flops=ACROSS_WORK[i],
            name="across",
        )
        last = totals[-1:]
    out = finish([v for v, _, _ in changes], totals, near, rows.shape)
    return jnp.swapaxes(out, 0, 1)[None]


def solution(mesh):
    in_specs = (
        P(("blk", "tp"), None),
        P(("blk", "tp"), None),
        P("blk", "tp", None, None),
        P("blk", "tp", None, None),
        P("blk", "tp", None, None),
    )
    out_specs = P("blk", "tp", None, None)
    return jax.shard_map(
        on_device, mesh=mesh, in_specs=in_specs, out_specs=out_specs, check_vma=False
    )
```

```python
import functools

import jax
import jax.numpy as jnp
from jax import lax
from jax.experimental import pallas as pl
from jax.experimental.pallas import tpu as pltpu
from jax.sharding import PartitionSpec as P

STEP = 10
CORRECT_ONE = 1.0 - 0.9**STEP
CORRECT_TWO = 1.0 - 0.95**STEP
HALF = jnp.bfloat16
FULL = jnp.float32
ORDER = (2, 1, 0)
AHEAD = 2
STILL_BY = 0
PIECES = (6, 5, 5)
NEAR_WORK = 5_000_000_000
PAIR_WORK = 20_000_000_000
AHEAD_WORK = 20_000_000_000
ACROSS_WORK = (20_000_000_000, 2_000_000_000, 2_000_000_000, 30_000_000_000)
FAR_WORK = 20_000_000_000


def neighbour(block, side):
    count = lax.axis_size("blk")
    if count % 2:
        route = [((i + 1 - 2 * side) % count, i) for i in range(count)]
    else:
        route = [((side + i) % count, (side + i + 1) % count) for i in range(0, count, 2)]
        route += [(j, i) for i, j in route]
    return lax.ppermute(block, "blk", route)


def adam_step(moment_one, moment_two):
    return moment_one / CORRECT_ONE / (jnp.sqrt(moment_two / CORRECT_TWO) + 1e-08)


def into_units(matrix, values):
    return lax.dot_general(matrix, values, (((1,), (1,)), ((), ())), preferred_element_type=FULL)


def over_tokens(terms, values):
    return lax.dot_general(terms, values, (((1,), (0,)), ((), ())), preferred_element_type=FULL)


def forward_terms(xs, gate_rows, upper_rows):
    scale = xs.shape[1] ** (-0.5)
    gate = into_units(gate_rows, xs) * scale
    upper = into_units(upper_rows, xs) * scale
    sigma = 1.0 / (1.0 + jnp.exp(-gate))
    swish = gate * sigma
    return (swish * upper).astype(HALF), swish, upper * sigma * (1.0 + gate * (1.0 - sigma))


def backward_terms(cots, down_rows, swish, slope, scale):
    back = into_units(down_rows, cots) * scale
    return (back * slope).astype(HALF), (back * swish).astype(HALF)


def unit_grads(xs, cots, rows, scale):
    hidden, swish, slope = forward_terms(xs, rows[0], rows[1])
    dgate, dupper = backward_terms(cots, rows[2], swish, slope, scale)
    width_scale = xs.shape[1] ** (-0.5)
    return jnp.stack(
        [
            over_tokens(dgate, xs) * width_scale,
            over_tokens(dupper, xs) * width_scale,
            over_tokens(hidden, cots) * scale,
        ]
    )


def call(kernel, outs, ins, after=(), flops=0, name=None):
    count = len(ins)

    def body(*refs):
        kernel(*refs[:count], *refs[count + len(after) :])

    return pl.pallas_call(
        body,
        out_shape=outs,
        in_specs=[pl.BlockSpec(memory_space=pltpu.VMEM)] * count
        + [pl.BlockSpec(memory_space=pl.ANY)] * len(after),
        out_specs=[pl.BlockSpec(memory_space=pltpu.VMEM)] * len(outs),
        cost_estimate=pl.CostEstimate(flops=flops, bytes_accessed=0, transcendentals=0),
        compiler_params=pltpu.CompilerParams(vmem_limit_bytes=32 * 2**20),
        name=name,
    )(*ins, *after)


def array(shape, dtype):
    return jax.ShapeDtypeStruct(shape, dtype)


def near_forward(*refs):
    *shards, rows, hidden, swish, slope = refs
    size = shards[0].shape[0]
    for i, xs in enumerate(shards):
        place = pl.ds(i * size, size)
        hidden[:, place], swish[:, place], slope[:, place] = forward_terms(
            xs[...], rows[0], rows[1]
        )


def joined(*parts):
    return jnp.concatenate([v[...] for v in parts], axis=1)


def inner_forward(*refs):
    near_forward(*refs[:-1])
    rows, top = refs[2], refs[-1]
    top[...] = rows[:2]


def near_backward(
    own_x, inner_x, pair_x, own_g, inner_g, pair_g,
    rows, hidden, swish, slope, pair_hidden, pair_swish, pair_slope, grads, more, *, scale
):
    size, width = own_x.shape
    more[...] = pair_g[:, width - more.shape[1] :]
    totals = [0.0, 0.0, 0.0]
    first, second = pl.ds(0, size), pl.ds(size, size)
    shards = (
        (own_x, own_g[...], hidden[:, first], swish[:, first], slope[:, first]),
        (inner_x, inner_g[...], hidden[:, second], swish[:, second], slope[:, second]),
        (pair_x, pair_g[...], pair_hidden[...], pair_swish[...], pair_slope[...]),
    )
    for xs, cots, hid, swi, slo in shards:
        dgate, dupper = backward_terms(cots, rows[2], swi, slo, scale)
        totals[0] += over_tokens(dgate, xs[...])
        totals[1] += over_tokens(dupper, xs[...])
        totals[2] += over_tokens(hid, cots)
    for k in range(3):
        grads[k] = totals[k] * (scale if k == 2 else width ** (-0.5))


def ahead_forward(inner_x, far_x, rows, pair_top, *terms):
    far_hidden, far_swish, far_slope, hidden, swish, slope = terms
    size = inner_x.shape[0]
    for i, xs in enumerate((inner_x, far_x)):
        place = pl.ds(i * size, size)
        hidden[:, place], swish[:, place], slope[:, place] = forward_terms(
            xs[...], pair_top[0], pair_top[1]
        )
    far_hidden[...], far_swish[...], far_slope[...] = forward_terms(far_x[...], rows[0], rows[1])


def ahead_backward(inner_g, pair_low, swish, slope, dgate, dupper, *, scale):
    size = inner_g.shape[0]
    dgate[...], dupper[...] = backward_terms(
        inner_g[...], pair_low[...], swish[:, :size], slope[:, :size], scale
    )


def pair_first(inner_x, inner_g, far_g, hidden, sent, *, scale):
    size = inner_x.shape[0]
    cut = sent.shape[1]
    total = over_tokens(hidden[:, :size], inner_g[:, :cut])
    total += over_tokens(hidden[:, size:], far_g[...])
    sent[...] = (total * scale).astype(HALF)


def pair_rest(
    inner_x, far_x, inner_g, far_g, more_g, pair_low, hidden, swish, slope, dgate, dupper,
    second, third, last, *, cut, scale
):
    size, width = inner_x.shape
    width_scale = width ** (-0.5)
    total = over_tokens(hidden[:, :size], inner_g[:, cut:])
    total += over_tokens(hidden[:, size:], more_g[...])
    columns = [(total * scale).astype(HALF)]
    far_terms = backward_terms(
        joined(far_g, more_g), pair_low[...], swish[:, size:], slope[:, size:], scale
    )
    for near, far in zip((dupper, dgate), far_terms[::-1]):
        total = over_tokens(near[...], inner_x[...]) + over_tokens(far, far_x[...])
        columns.append((total * width_scale).astype(HALF))
    columns = jnp.concatenate(columns, axis=1)
    start = 0
    for part in (second, third, last):
        part[...] = columns[:, start : start + part.shape[1]]
        start += part.shape[1]


def far_backward(far_x, far_g, more_g, rows, hidden, swish, slope, near, grads, *, scale):
    width_scale = far_x.shape[1] ** (-0.5)
    cots = joined(far_g, more_g)
    dgate, dupper = backward_terms(cots, rows[2], swish[...], slope[...], scale)
    grads[0] = near[0] + over_tokens(dgate, far_x[...]) * width_scale
    grads[1] = near[1] + over_tokens(dupper, far_x[...]) * width_scale
    grads[2] = near[2] + over_tokens(hidden[...], cots) * scale


def cut_columns(whole, rows, part, low):
    part[...] = whole[:, : part.shape[1]]
    low[...] = rows[2]


def line_of_four(tokens, cots, sent_cots, cuts, rows, still, scale):
    pairs = [(0, 1), (1, 0), (2, 3), (3, 2)]
    middle = [(1, 2), (2, 1)]
    units, width = rows.shape[1:]
    size = tokens.shape[0]

    def send(block, route):
        return lax.ppermute(block, "tp", route)

    inner_x = send(tokens, middle)
    pair_x = send(tokens, pairs)
    inner_g = send(cots, middle)
    pair_g = send(sent_cots, pairs)
    far_x = send(pair_x, middle)
    *near_terms, top = call(
        inner_forward,
        [array((units, 2 * size), t) for t in (HALF, FULL, FULL)]
        + [array((2, units, width), HALF)],
        (tokens, inner_x, rows),
        after=(still,),
        flops=NEAR_WORK,
        name="near_forward",
    )
    pair_top = send(top, pairs)
    pair_terms = call(
        near_forward,
        [array((units, size), t) for t in (HALF, FULL, FULL)],
        (pair_x, rows),
        after=near_terms[:1],
        flops=PAIR_WORK,
        name="pair_forward",
    )
    pair_part, low = call(
        cut_columns,
        [array((size, cuts[0]), HALF), array((units, width), HALF)],
        (pair_g, rows),
        after=pair_terms[:1],
        name="cut",
    )
    pair_low = send(low, pairs)
    near, pair_more = call(
        functools.partial(near_backward, scale=scale),
        [array((3, units, width), FULL), array((size, cuts[1]), HALF)],
        (tokens, inner_x, pair_x, cots, inner_g, pair_g, rows, *near_terms, *pair_terms),
        after=(pair_part,),
        name="near_backward",
    )
    far_gs = [send(v, middle) for v in (pair_part, pair_more)]
    ahead = call(
        ahead_forward,
        [array((units, size), t) for t in (HALF, FULL, FULL)]
        + [array((units, 2 * size), t) for t in (HALF, FULL, FULL)],
        (inner_x, far_x, rows, pair_top),
        after=(near,),
        flops=AHEAD_WORK,
        name="ahead_forward",
    )
    far_terms, (hidden, swish, slope) = ahead[:3], ahead[3:]
    sizes = [width * v // (7 * 128) * 128 for v in PIECES]
    sizes.append(3 * width - sum(sizes))
    cut, more = sizes[0], sizes[0] + sizes[1] - width
    ends = width - sizes[3]
    first = call(
        functools.partial(pair_first, scale=scale),
        [array((units, sizes[0]), HALF)],
        (inner_x, inner_g, far_gs[0], hidden),
        name="pair_first",
    )[0]
    dgate, dupper = call(
        functools.partial(ahead_backward, scale=scale),
        [array((units, size), HALF)] * 2,
        (inner_g, pair_low, swish, slope),
        after=(first,),
        name="ahead_backward",
    )
    grads = call(
        functools.partial(far_backward, scale=scale),
        [array((3, units, width), FULL)],
        (far_x, *far_gs, rows, *far_terms, near),
        after=(dgate,),
        flops=FAR_WORK,
        name="far_backward",
    )[0]
    second, third, last = call(
        functools.partial(pair_rest, cut=cut, scale=scale),
        [array((units, v), HALF) for v in sizes[1:]],
        (inner_x, far_x, inner_g, *far_gs, pair_low, hidden, swish, slope, dgate, dupper),
        after=(grads,),
        name="pair_rest",
    )
    pieces = [
        ([(2, 0, cut)], first),
        ([(2, cut, width - cut), (1, 0, more)], second),
        ([(1, more, width - more), (0, 0, ends)], third),
        ([(0, ends, sizes[3])], last),
    ]
    pieces = [(tuple(v for v in piece if v[2]), parts) for piece, parts in pieces]
    return grads, pieces, lambda block: send(block, pairs)


def gathered(tokens, cots, rows, scale):
    return unit_grads(
        lax.all_gather(tokens, "tp", axis=0, tiled=True),
        lax.all_gather(cots, "tp", axis=0, tiled=True),
        rows,
        scale,
    )


def still_kernel(rows, first, second, cots, still, step, same_cots):
    master = rows[...].astype(FULL)
    total = adam_step(0.9 * first[...].astype(FULL), 0.95 * second[...].astype(FULL))
    step[...] = total
    still[...] = master - 0.1 * (total + 0.1 * master)

    @pl.when(pl.program_id(0) == 0)
    def _():
        same_cots[...] = cots[...]


def still_values(rows, first, second, cots):
    slab = pl.BlockSpec((1, *rows.shape[1:]), lambda k: (k, 0, 0))
    whole = pl.BlockSpec(cots.shape, lambda k: (0, 0))
    return pl.pallas_call(
        still_kernel,
        grid=(3,),
        out_shape=[array(rows.shape, FULL)] * 2 + [array(cots.shape, cots.dtype)],
        in_specs=[slab] * 3 + [whole],
        out_specs=[slab] * 2 + [whole],
        compiler_params=pltpu.CompilerParams(vmem_limit_bytes=32 * 2**20),
        name="still",
    )(rows, first, second, cots)


def spans(piece):
    start = 0
    for k, first, size in piece:
        yield k, pl.ds(first, size), pl.ds(start, size)
        start += size


def columns_of(piece):
    return sum(size for _, _, size in piece)


def change_kernel(grads, still, still_step, first, second, *rest, piece, parts, ready):
    came, rest = rest[:parts], rest[parts:]
    ready, (updated, sent, *passed) = rest[:ready], rest[ready:]
    for block, same in zip(ready, passed):
        same[...] = block[...]
    for k, place, here in spans(piece):
        grad = grads[k, :, place]
        for part in came:
            grad = grad + part[:, here].astype(FULL)
        moment_one = 0.9 * first[k, :, place].astype(FULL) + 0.1 * grad
        moment_two = 0.95 * second[k, :, place].astype(FULL) + 0.05 * grad * grad
        total = 0.1 * (still_step[k, :, place] - adam_step(moment_one, moment_two))
        updated[:, here] = still[k, :, place] + total
        sent[:, here] = total.astype(HALF)


def change_of(piece, grads, still, still_step, first, second, came, ready, after):
    shape = (grads.shape[1], columns_of(piece))
    return call(
        functools.partial(change_kernel, piece=piece, parts=len(came), ready=len(ready)),
        [array(shape, FULL), array(shape, HALF)] + [array(v.shape, v.dtype) for v in ready],
        (grads, still, still_step, first, second, *came, *ready),
        after=after,
        name="change",
    )


def join_kernel(*refs):
    *blocks, joint = refs
    start = 0
    for block in blocks:
        joint[:, pl.ds(start, block.shape[1])] = block[...]
        start += block.shape[1]


def across_kernel(updated, still, far, total, *, piece):
    for k, place, here in spans(piece):
        total[:, here] = updated[:, here] + still[k, :, place] + far[:, here].astype(FULL)


def finish_kernel(*refs, pieces, bands):
    *parts, near, out, total, done = refs
    units = near.shape[0]
    copies, start = [], 0
    for part, piece in zip(parts, pieces):
        for k, place, here in spans(piece):
            there = pl.ds(start, place.size)
            for i, band in enumerate(bands):
                rows = pl.ds(band, (*bands, units)[i + 1] - band)
                total[rows, there] = (part[rows, here] + near[rows, there]) / 3.0
                copies.append(
                    pltpu.make_async_copy(
                        total.at[rows, there], out.at[k, rows, place], done.at[len(copies)]
                    )
                )
                copies[-1].start()
            start += place.size
    for copy in copies:
        copy.wait()


def finish(pieces, parts, near, shape):
    units = shape[1]
    bands = (0, units // 32 * 16)
    vmem = pl.BlockSpec(memory_space=pltpu.VMEM)
    return pl.pallas_call(
        functools.partial(finish_kernel, pieces=pieces, bands=bands),
        out_shape=array(shape, FULL),
        in_specs=[vmem] * (len(parts) + 1),
        out_specs=pl.BlockSpec(memory_space=pl.ANY),
        scratch_shapes=[
            pltpu.VMEM(near.shape, FULL),
            pltpu.SemaphoreType.DMA((2 * sum(len(v) for v in pieces),)),
        ],
        cost_estimate=pl.CostEstimate(flops=0, bytes_accessed=0, transcendentals=0),
        compiler_params=pltpu.CompilerParams(vmem_limit_bytes=32 * 2**20),
        name="finish",
    )(*parts, near)


def on_device(tokens, cotangent, weights, first_moment, second_moment):
    rows, first, second = (
        jnp.swapaxes(v[0], 0, 1) for v in (weights, first_moment, second_moment)
    )
    scale = (rows.shape[1] * lax.axis_size("tp")) ** (-0.5)
    width = rows.shape[2]
    cuts = (width * PIECES[0] // (7 * 128) * 128,)
    cuts += (width - cuts[0],)
    still, still_step, sent_cots = still_values(rows, first, second, cotangent)
    still_far = neighbour(still, 1)
    if lax.axis_size("tp") == 4:
        grads, pieces, send = line_of_four(
            tokens, cotangent, sent_cots, cuts, rows, still, scale
        )
    else:
        grads = gathered(tokens, cotangent, rows, scale)
        pieces = [([(k, 0, rows.shape[2])], None) for k in ORDER]
    came = [[] if v is None else [send(v)] for _, v in pieces[:AHEAD]]
    changes, last = [], ()
    for i, (piece, _) in enumerate(pieces):
        ready = [v for _, v in pieces[i + AHEAD : i + AHEAD + 1] if v is not None]
        updated, sent, *ready = change_of(
            piece, grads, still, still_step, first, second, came[i], ready, last
        )
        came.append([send(v) for v in ready])
        changes.append((piece, updated, neighbour(sent, 1)))
        last = (sent, still_far) if i == STILL_BY else (sent,)
    updates = [v for _, v, _ in changes]
    joint = call(
        join_kernel, [array((rows.shape[1], 3 * width), FULL)], updates, name="join"
    )[0]
    near = neighbour(joint, 0)
    totals, last = [], (joint,)
    for i, (piece, updated, far) in enumerate(changes):
        totals += call(
            functools.partial(across_kernel, piece=piece),
            [array(updated.shape, FULL)],
            (updated, still_far, far),
            after=last,
            flops=ACROSS_WORK[i],
            name="across",
        )
        last = totals[-1:]
    out = finish([v for v, _, _ in changes], totals, near, rows.shape)
    return jnp.swapaxes(out, 0, 1)[None]


def solution(mesh):
    in_specs = (
        P(("blk", "tp"), None),
        P(("blk", "tp"), None),
        P("blk", "tp", None, None),
        P("blk", "tp", None, None),
        P("blk", "tp", None, None),
    )
    out_specs = P("blk", "tp", None, None)
    return jax.shard_map(
        on_device, mesh=mesh, in_specs=in_specs, out_specs=out_specs, check_vma=False
    )
```

```python
import functools

import jax
import jax.numpy as jnp
from jax import lax
from jax.experimental import pallas as pl
from jax.experimental.pallas import tpu as pltpu
from jax.sharding import PartitionSpec as P

STEP = 10
CORRECT_ONE = 1.0 - 0.9**STEP
CORRECT_TWO = 1.0 - 0.95**STEP
HALF = jnp.bfloat16
FULL = jnp.float32
ORDER = (2, 1, 0)
AHEAD = 2
STILL_BY = 0
PIECES = (5, 5, 6)
NEAR_WORK = 5_000_000_000
PAIR_WORK = 20_000_000_000
AHEAD_WORK = 20_000_000_000
ACROSS_WORK = (20_000_000_000, 2_000_000_000, 2_000_000_000, 30_000_000_000)
FAR_WORK = 0
CHANGE_WORK = (0, 5_000_000_000, 5_000_000_000, 0)


def neighbour(block, side):
    count = lax.axis_size("blk")
    if count % 2:
        route = [((i + 1 - 2 * side) % count, i) for i in range(count)]
    else:
        route = [((side + i) % count, (side + i + 1) % count) for i in range(0, count, 2)]
        route += [(j, i) for i, j in route]
    return lax.ppermute(block, "blk", route)


def adam_step(moment_one, moment_two):
    return moment_one / CORRECT_ONE / (jnp.sqrt(moment_two / CORRECT_TWO) + 1e-08)


def into_units(matrix, values):
    return lax.dot_general(matrix, values, (((1,), (1,)), ((), ())), preferred_element_type=FULL)


def over_tokens(terms, values):
    return lax.dot_general(terms, values, (((1,), (0,)), ((), ())), preferred_element_type=FULL)


def forward_terms(xs, gate_rows, upper_rows):
    scale = xs.shape[1] ** (-0.5)
    gate = into_units(gate_rows, xs) * scale
    upper = into_units(upper_rows, xs) * scale
    sigma = 1.0 / (1.0 + jnp.exp(-gate))
    swish = gate * sigma
    return (swish * upper).astype(HALF), swish, upper * sigma * (1.0 + gate * (1.0 - sigma))


def backward_terms(cots, down_rows, swish, slope, scale):
    back = into_units(down_rows, cots) * scale
    return (back * slope).astype(HALF), (back * swish).astype(HALF)


def unit_grads(xs, cots, rows, scale):
    hidden, swish, slope = forward_terms(xs, rows[0], rows[1])
    dgate, dupper = backward_terms(cots, rows[2], swish, slope, scale)
    width_scale = xs.shape[1] ** (-0.5)
    return jnp.stack(
        [
            over_tokens(dgate, xs) * width_scale,
            over_tokens(dupper, xs) * width_scale,
            over_tokens(hidden, cots) * scale,
        ]
    )


def call(kernel, outs, ins, after=(), flops=0, name=None):
    count = len(ins)

    def body(*refs):
        kernel(*refs[:count], *refs[count + len(after) :])

    return pl.pallas_call(
        body,
        out_shape=outs,
        in_specs=[pl.BlockSpec(memory_space=pltpu.VMEM)] * count
        + [pl.BlockSpec(memory_space=pl.ANY)] * len(after),
        out_specs=[pl.BlockSpec(memory_space=pltpu.VMEM)] * len(outs),
        cost_estimate=pl.CostEstimate(flops=flops, bytes_accessed=0, transcendentals=0),
        compiler_params=pltpu.CompilerParams(vmem_limit_bytes=32 * 2**20),
        name=name,
    )(*ins, *after)


def array(shape, dtype):
    return jax.ShapeDtypeStruct(shape, dtype)


def near_forward(*refs):
    *shards, rows, hidden, swish, slope = refs
    size = shards[0].shape[0]
    for i, xs in enumerate(shards):
        place = pl.ds(i * size, size)
        hidden[:, place], swish[:, place], slope[:, place] = forward_terms(
            xs[...], rows[0], rows[1]
        )


def joined(*parts):
    return jnp.concatenate([v[...] for v in parts], axis=1)


def inner_forward(*refs):
    near_forward(*refs[:-1])
    rows, top = refs[2], refs[-1]
    top[...] = rows[:2]


def near_backward(
    own_x, inner_x, pair_x, own_g, inner_g, pair_g,
    rows, hidden, swish, slope, pair_hidden, pair_swish, pair_slope, grads, *, scale
):
    size, width = own_x.shape
    totals = [0.0, 0.0, 0.0]
    first, second = pl.ds(0, size), pl.ds(size, size)
    shards = (
        (own_x, own_g[...], hidden[:, first], swish[:, first], slope[:, first]),
        (inner_x, inner_g[...], hidden[:, second], swish[:, second], slope[:, second]),
        (pair_x, pair_g[...], pair_hidden[...], pair_swish[...], pair_slope[...]),
    )
    for xs, cots, hid, swi, slo in shards:
        dgate, dupper = backward_terms(cots, rows[2], swi, slo, scale)
        totals[0] += over_tokens(dgate, xs[...])
        totals[1] += over_tokens(dupper, xs[...])
        totals[2] += over_tokens(hid, cots)
    for k in range(3):
        grads[k] = totals[k] * (scale if k == 2 else width ** (-0.5))


def far_forward(far_x, rows, pair_g, hidden, swish, slope, more):
    more[...] = pair_g[:, pair_g.shape[1] - more.shape[1] :]
    hidden[...], swish[...], slope[...] = forward_terms(far_x[...], rows[0], rows[1])


def ahead_backward(inner_g, pair_low, swish, slope, dgate, dupper, *, scale):
    size = inner_g.shape[0]
    dgate[...], dupper[...] = backward_terms(
        inner_g[...], pair_low[...], swish[:, :size], slope[:, :size], scale
    )


def pair_first(inner_x, inner_g, far_g, hidden, sent, *, scale):
    size = inner_x.shape[0]
    cut = sent.shape[1]
    total = over_tokens(hidden[:, :size], inner_g[:, :cut])
    total += over_tokens(hidden[:, size:], far_g[...])
    sent[...] = (total * scale).astype(HALF)


def pair_rest(
    inner_x, far_x, inner_g, far_g, more_g, pair_low, hidden, swish, slope, dgate, dupper,
    second, third, last, *, cut, scale
):
    size, width = inner_x.shape
    width_scale = width ** (-0.5)
    total = over_tokens(hidden[:, :size], inner_g[:, cut:])
    total += over_tokens(hidden[:, size:], more_g[...])
    columns = [(total * scale).astype(HALF)]
    far_terms = backward_terms(
        joined(far_g, more_g), pair_low[...], swish[:, size:], slope[:, size:], scale
    )
    for near, far in zip((dupper, dgate), far_terms[::-1]):
        total = over_tokens(near[...], inner_x[...]) + over_tokens(far, far_x[...])
        columns.append((total * width_scale).astype(HALF))
    columns = jnp.concatenate(columns, axis=1)
    start = 0
    for part in (second, third, last):
        part[...] = columns[:, start : start + part.shape[1]]
        start += part.shape[1]


def far_backward(far_x, far_g, more_g, rows, hidden, swish, slope, near, grads, *, scale):
    width_scale = far_x.shape[1] ** (-0.5)
    cots = joined(far_g, more_g)
    dgate, dupper = backward_terms(cots, rows[2], swish[...], slope[...], scale)
    grads[0] = near[0] + over_tokens(dgate, far_x[...]) * width_scale
    grads[1] = near[1] + over_tokens(dupper, far_x[...]) * width_scale
    grads[2] = near[2] + over_tokens(hidden[...], cots) * scale


def cut_columns(whole, rows, part, low):
    part[...] = whole[:, : part.shape[1]]
    low[...] = rows[2]


def line_of_four(tokens, cots, sent_cots, cuts, rows, still, scale):
    pairs = [(0, 1), (1, 0), (2, 3), (3, 2)]
    middle = [(1, 2), (2, 1)]
    units, width = rows.shape[1:]
    size = tokens.shape[0]

    def send(block, route):
        return lax.ppermute(block, "tp", route)

    inner_x = send(tokens, middle)
    pair_x = send(tokens, pairs)
    inner_g = send(cots, middle)
    pair_g = send(sent_cots, pairs)
    far_x = send(pair_x, middle)
    *near_terms, top = call(
        inner_forward,
        [array((units, 2 * size), t) for t in (HALF, FULL, FULL)]
        + [array((2, units, width), HALF)],
        (tokens, inner_x, rows),
        after=(still,),
        flops=NEAR_WORK,
        name="near_forward",
    )
    pair_top = send(top, pairs)
    pair_terms = call(
        near_forward,
        [array((units, size), t) for t in (HALF, FULL, FULL)],
        (pair_x, rows),
        after=near_terms[:1],
        flops=PAIR_WORK,
        name="pair_forward",
    )
    pair_part, low = call(
        cut_columns,
        [array((size, cuts[0]), HALF), array((units, width), HALF)],
        (pair_g, rows),
        after=pair_terms[:1],
        name="cut",
    )
    pair_low = send(low, pairs)
    near = call(
        functools.partial(near_backward, scale=scale),
        [array((3, units, width), FULL)],
        (tokens, inner_x, pair_x, cots, inner_g, pair_g, rows, *near_terms, *pair_terms),
        after=(pair_part,),
        name="near_backward",
    )[0]
    *far_terms, pair_more = call(
        far_forward,
        [array((units, size), t) for t in (HALF, FULL, FULL)]
        + [array((size, cuts[1]), HALF)],
        (far_x, rows, pair_g),
        after=(near,),
        name="far_forward",
    )
    far_gs = [send(v, middle) for v in (pair_part, pair_more)]
    hidden, swish, slope = call(
        near_forward,
        [array((units, 2 * size), t) for t in (HALF, FULL, FULL)],
        (inner_x, far_x, pair_top),
        after=(pair_more,),
        flops=AHEAD_WORK,
        name="ahead_forward",
    )
    sizes = [width * v // (7 * 128) * 128 for v in PIECES]
    sizes.append(3 * width - sum(sizes))
    cut, more = sizes[0], sizes[0] + sizes[1] - width
    ends = width - sizes[3]
    first = call(
        functools.partial(pair_first, scale=scale),
        [array((units, sizes[0]), HALF)],
        (inner_x, inner_g, far_gs[0], hidden),
        name="pair_first",
    )[0]
    dgate, dupper = call(
        functools.partial(ahead_backward, scale=scale),
        [array((units, size), HALF)] * 2,
        (inner_g, pair_low, swish, slope),
        after=(first,),
        name="ahead_backward",
    )
    grads = call(
        functools.partial(far_backward, scale=scale),
        [array((3, units, width), FULL)],
        (far_x, *far_gs, rows, *far_terms, near),
        after=(dgate,),
        flops=FAR_WORK,
        name="far_backward",
    )[0]
    second, third, last = call(
        functools.partial(pair_rest, cut=cut, scale=scale),
        [array((units, v), HALF) for v in sizes[1:]],
        (inner_x, far_x, inner_g, *far_gs, pair_low, hidden, swish, slope, dgate, dupper),
        after=(grads,),
        name="pair_rest",
    )
    pieces = [
        ([(2, 0, cut)], first),
        ([(2, cut, width - cut), (1, 0, more)], second),
        ([(1, more, width - more), (0, 0, ends)], third),
        ([(0, ends, sizes[3])], last),
    ]
    pieces = [(tuple(v for v in piece if v[2]), parts) for piece, parts in pieces]
    return grads, pieces, lambda block: send(block, pairs)


def gathered(tokens, cots, rows, scale):
    return unit_grads(
        lax.all_gather(tokens, "tp", axis=0, tiled=True),
        lax.all_gather(cots, "tp", axis=0, tiled=True),
        rows,
        scale,
    )


def still_kernel(rows, first, second, cots, still, step, same_cots):
    master = rows[...].astype(FULL)
    total = adam_step(0.9 * first[...].astype(FULL), 0.95 * second[...].astype(FULL))
    step[...] = total
    still[...] = master - 0.1 * (total + 0.1 * master)

    @pl.when(pl.program_id(0) == 0)
    def _():
        same_cots[...] = cots[...]


def still_values(rows, first, second, cots):
    slab = pl.BlockSpec((1, *rows.shape[1:]), lambda k: (k, 0, 0))
    whole = pl.BlockSpec(cots.shape, lambda k: (0, 0))
    return pl.pallas_call(
        still_kernel,
        grid=(3,),
        out_shape=[array(rows.shape, FULL)] * 2 + [array(cots.shape, cots.dtype)],
        in_specs=[slab] * 3 + [whole],
        out_specs=[slab] * 2 + [whole],
        compiler_params=pltpu.CompilerParams(vmem_limit_bytes=32 * 2**20),
        name="still",
    )(rows, first, second, cots)


def spans(piece):
    start = 0
    for k, first, size in piece:
        yield k, pl.ds(first, size), pl.ds(start, size)
        start += size


def columns_of(piece):
    return sum(size for _, _, size in piece)


def change_kernel(grads, still, still_step, first, second, *rest, piece, parts, ready):
    came, rest = rest[:parts], rest[parts:]
    ready, (updated, sent, *passed) = rest[:ready], rest[ready:]
    for block, same in zip(ready, passed):
        same[...] = block[...]
    for k, place, here in spans(piece):
        grad = grads[k, :, place]
        for part in came:
            grad = grad + part[:, here].astype(FULL)
        moment_one = 0.9 * first[k, :, place].astype(FULL) + 0.1 * grad
        moment_two = 0.95 * second[k, :, place].astype(FULL) + 0.05 * grad * grad
        total = 0.1 * (still_step[k, :, place] - adam_step(moment_one, moment_two))
        updated[:, here] = still[k, :, place] + total
        sent[:, here] = total.astype(HALF)


def change_of(piece, grads, still, still_step, first, second, came, ready, after, flops):
    shape = (grads.shape[1], columns_of(piece))
    return call(
        functools.partial(change_kernel, piece=piece, parts=len(came), ready=len(ready)),
        [array(shape, FULL), array(shape, HALF)] + [array(v.shape, v.dtype) for v in ready],
        (grads, still, still_step, first, second, *came, *ready),
        after=after,
        flops=flops,
        name="change",
    )


def join_kernel(*refs):
    *blocks, joint = refs
    start = 0
    for block in blocks:
        joint[:, pl.ds(start, block.shape[1])] = block[...]
        start += block.shape[1]


def across_kernel(updated, still, far, total, *, piece):
    for k, place, here in spans(piece):
        total[:, here] = updated[:, here] + still[k, :, place] + far[:, here].astype(FULL)


def across_of(i, change, still, after):
    piece, updated, far = change
    return call(
        functools.partial(across_kernel, piece=piece),
        [array(updated.shape, FULL)],
        (updated, still, far),
        after=after,
        flops=ACROSS_WORK[i],
        name="across",
    )[0]


def finish_kernel(*refs, pieces, bands):
    *parts, near, out, total, done = refs
    units = near.shape[0]
    copies, start = [], 0
    for part, piece in zip(parts, pieces):
        for k, place, here in spans(piece):
            there = pl.ds(start, place.size)
            for i, band in enumerate(bands):
                rows = pl.ds(band, (*bands, units)[i + 1] - band)
                total[rows, there] = (part[rows, here] + near[rows, there]) / 3.0
                copies.append(
                    pltpu.make_async_copy(
                        total.at[rows, there], out.at[k, rows, place], done.at[len(copies)]
                    )
                )
                copies[-1].start()
            start += place.size
    for copy in copies:
        copy.wait()


def finish(pieces, parts, near, shape):
    units = shape[1]
    bands = (0, units // 32 * 16)
    vmem = pl.BlockSpec(memory_space=pltpu.VMEM)
    return pl.pallas_call(
        functools.partial(finish_kernel, pieces=pieces, bands=bands),
        out_shape=array(shape, FULL),
        in_specs=[vmem] * (len(parts) + 1),
        out_specs=pl.BlockSpec(memory_space=pl.ANY),
        scratch_shapes=[
            pltpu.VMEM(near.shape, FULL),
            pltpu.SemaphoreType.DMA((2 * sum(len(v) for v in pieces),)),
        ],
        cost_estimate=pl.CostEstimate(flops=0, bytes_accessed=0, transcendentals=0),
        compiler_params=pltpu.CompilerParams(vmem_limit_bytes=32 * 2**20),
        name="finish",
    )(*parts, near)


def on_device(tokens, cotangent, weights, first_moment, second_moment):
    rows, first, second = (
        jnp.swapaxes(v[0], 0, 1) for v in (weights, first_moment, second_moment)
    )
    scale = (rows.shape[1] * lax.axis_size("tp")) ** (-0.5)
    width = rows.shape[2]
    cuts = (width * PIECES[0] // (7 * 128) * 128,)
    cuts += (width - cuts[0],)
    still, still_step, sent_cots = still_values(rows, first, second, cotangent)
    still_far = neighbour(still, 1)
    if lax.axis_size("tp") == 4:
        grads, pieces, send = line_of_four(
            tokens, cotangent, sent_cots, cuts, rows, still, scale
        )
    else:
        grads = gathered(tokens, cotangent, rows, scale)
        pieces = [([(k, 0, rows.shape[2])], None) for k in ORDER]
    count = len(pieces)
    came = [[] if v is None else [send(v)] for _, v in pieces[:AHEAD]]
    changes, last = [], ()
    for i, (piece, _) in enumerate(pieces):
        ready = [v for _, v in pieces[i + AHEAD : i + AHEAD + 1] if v is not None]
        updated, sent, *ready = change_of(
            piece,
            grads,
            still,
            still_step,
            first,
            second,
            came[i],
            ready,
            last,
            CHANGE_WORK[i],
        )
        came.append([send(v) for v in ready])
        changes.append((piece, updated, neighbour(sent, 1)))
        last = (sent, still_far) if i == STILL_BY else (sent,)
        if i == count - 2:
            totals = [across_of(0, changes[0], still_far, last)]
            last += (totals[0],)
    updates = [v for _, v, _ in changes]
    joint = call(
        join_kernel, [array((rows.shape[1], 3 * width), FULL)], updates, name="join"
    )[0]
    near = neighbour(joint, 0)
    for i in range(1, count):
        totals.append(across_of(i, changes[i], still_far, (joint, totals[-1])))
    out = finish([v for v, _, _ in changes], totals, near, rows.shape)
    return jnp.swapaxes(out, 0, 1)[None]


def solution(mesh):
    in_specs = (
        P(("blk", "tp"), None),
        P(("blk", "tp"), None),
        P("blk", "tp", None, None),
        P("blk", "tp", None, None),
        P("blk", "tp", None, None),
    )
    out_specs = P("blk", "tp", None, None)
    return jax.shard_map(
        on_device, mesh=mesh, in_specs=in_specs, out_specs=out_specs, check_vma=False
    )
```

```python
import functools

import jax
import jax.numpy as jnp
from jax import lax
from jax.experimental import pallas as pl
from jax.experimental.pallas import tpu as pltpu
from jax.sharding import PartitionSpec as P

STEP = 10
CORRECT_ONE = 1.0 - 0.9**STEP
CORRECT_TWO = 1.0 - 0.95**STEP
HALF = jnp.bfloat16
FULL = jnp.float32
ORDER = (2, 1, 0)
AHEAD = 2
STILL_BY = 0
PIECES = (5, 5, 6)
NEAR_WORK = 5_000_000_000
PAIR_WORK = 20_000_000_000
AHEAD_WORK = 20_000_000_000
ACROSS_WORK = (20_000_000_000, 2_000_000_000, 60_000_000_000, 30_000_000_000)
FAR_WORK = 0
CHANGE_WORK = (0, 5_000_000_000, 5_000_000_000, 0)


def neighbour(block, side):
    count = lax.axis_size("blk")
    if count % 2:
        route = [((i + 1 - 2 * side) % count, i) for i in range(count)]
    else:
        route = [((side + i) % count, (side + i + 1) % count) for i in range(0, count, 2)]
        route += [(j, i) for i, j in route]
    return lax.ppermute(block, "blk", route)


def adam_step(moment_one, moment_two):
    return moment_one / CORRECT_ONE / (jnp.sqrt(moment_two / CORRECT_TWO) + 1e-08)


def into_units(matrix, values):
    return lax.dot_general(matrix, values, (((1,), (1,)), ((), ())), preferred_element_type=FULL)


def over_tokens(terms, values):
    return lax.dot_general(terms, values, (((1,), (0,)), ((), ())), preferred_element_type=FULL)


def forward_terms(xs, gate_rows, upper_rows):
    scale = xs.shape[1] ** (-0.5)
    gate = into_units(gate_rows, xs) * scale
    upper = into_units(upper_rows, xs) * scale
    sigma = 1.0 / (1.0 + jnp.exp(-gate))
    swish = gate * sigma
    return (swish * upper).astype(HALF), swish, upper * sigma * (1.0 + gate * (1.0 - sigma))


def backward_terms(cots, down_rows, swish, slope, scale):
    back = into_units(down_rows, cots) * scale
    return (back * slope).astype(HALF), (back * swish).astype(HALF)


def unit_grads(xs, cots, rows, scale):
    hidden, swish, slope = forward_terms(xs, rows[0], rows[1])
    dgate, dupper = backward_terms(cots, rows[2], swish, slope, scale)
    width_scale = xs.shape[1] ** (-0.5)
    return jnp.stack(
        [
            over_tokens(dgate, xs) * width_scale,
            over_tokens(dupper, xs) * width_scale,
            over_tokens(hidden, cots) * scale,
        ]
    )


def call(kernel, outs, ins, after=(), flops=0, name=None):
    count = len(ins)

    def body(*refs):
        kernel(*refs[:count], *refs[count + len(after) :])

    return pl.pallas_call(
        body,
        out_shape=outs,
        in_specs=[pl.BlockSpec(memory_space=pltpu.VMEM)] * count
        + [pl.BlockSpec(memory_space=pl.ANY)] * len(after),
        out_specs=[pl.BlockSpec(memory_space=pltpu.VMEM)] * len(outs),
        cost_estimate=pl.CostEstimate(flops=flops, bytes_accessed=0, transcendentals=0),
        compiler_params=pltpu.CompilerParams(vmem_limit_bytes=32 * 2**20),
        name=name,
    )(*ins, *after)


def array(shape, dtype):
    return jax.ShapeDtypeStruct(shape, dtype)


def near_forward(*refs):
    *shards, rows, hidden, swish, slope = refs
    size = shards[0].shape[0]
    for i, xs in enumerate(shards):
        place = pl.ds(i * size, size)
        hidden[:, place], swish[:, place], slope[:, place] = forward_terms(
            xs[...], rows[0], rows[1]
        )


def joined(*parts):
    return jnp.concatenate([v[...] for v in parts], axis=1)


def inner_forward(*refs):
    near_forward(*refs[:-1])
    rows, top = refs[2], refs[-1]
    top[...] = rows[:2]


def near_backward(
    own_x, inner_x, pair_x, own_g, inner_g, pair_g,
    rows, hidden, swish, slope, pair_hidden, pair_swish, pair_slope, grads, *, scale
):
    size, width = own_x.shape
    totals = [0.0, 0.0, 0.0]
    first, second = pl.ds(0, size), pl.ds(size, size)
    shards = (
        (own_x, own_g[...], hidden[:, first], swish[:, first], slope[:, first]),
        (inner_x, inner_g[...], hidden[:, second], swish[:, second], slope[:, second]),
        (pair_x, pair_g[...], pair_hidden[...], pair_swish[...], pair_slope[...]),
    )
    for xs, cots, hid, swi, slo in shards:
        dgate, dupper = backward_terms(cots, rows[2], swi, slo, scale)
        totals[0] += over_tokens(dgate, xs[...])
        totals[1] += over_tokens(dupper, xs[...])
        totals[2] += over_tokens(hid, cots)
    for k in range(3):
        grads[k] = totals[k] * (scale if k == 2 else width ** (-0.5))


def far_forward(far_x, rows, pair_g, hidden, swish, slope, more):
    more[...] = pair_g[:, pair_g.shape[1] - more.shape[1] :]
    hidden[...], swish[...], slope[...] = forward_terms(far_x[...], rows[0], rows[1])


def ahead_backward(inner_g, pair_low, swish, slope, dgate, dupper, *, scale):
    size = inner_g.shape[0]
    dgate[...], dupper[...] = backward_terms(
        inner_g[...], pair_low[...], swish[:, :size], slope[:, :size], scale
    )


def pair_first(inner_x, inner_g, far_g, hidden, sent, *, scale):
    size = inner_x.shape[0]
    cut = sent.shape[1]
    total = over_tokens(hidden[:, :size], inner_g[:, :cut])
    total += over_tokens(hidden[:, size:], far_g[...])
    sent[...] = (total * scale).astype(HALF)


def pair_rest(
    inner_x, far_x, inner_g, far_g, more_g, pair_low, hidden, swish, slope, dgate, dupper,
    second, third, last, *, cut, scale
):
    size, width = inner_x.shape
    width_scale = width ** (-0.5)
    total = over_tokens(hidden[:, :size], inner_g[:, cut:])
    total += over_tokens(hidden[:, size:], more_g[...])
    columns = [(total * scale).astype(HALF)]
    far_terms = backward_terms(
        joined(far_g, more_g), pair_low[...], swish[:, size:], slope[:, size:], scale
    )
    for near, far in zip((dupper, dgate), far_terms[::-1]):
        total = over_tokens(near[...], inner_x[...]) + over_tokens(far, far_x[...])
        columns.append((total * width_scale).astype(HALF))
    columns = jnp.concatenate(columns, axis=1)
    start = 0
    for part in (second, third, last):
        part[...] = columns[:, start : start + part.shape[1]]
        start += part.shape[1]


def far_backward(far_x, far_g, more_g, rows, hidden, swish, slope, near, grads, *, scale):
    width_scale = far_x.shape[1] ** (-0.5)
    cots = joined(far_g, more_g)
    dgate, dupper = backward_terms(cots, rows[2], swish[...], slope[...], scale)
    grads[0] = near[0] + over_tokens(dgate, far_x[...]) * width_scale
    grads[1] = near[1] + over_tokens(dupper, far_x[...]) * width_scale
    grads[2] = near[2] + over_tokens(hidden[...], cots) * scale


def cut_columns(whole, rows, part, low):
    part[...] = whole[:, : part.shape[1]]
    low[...] = rows[2]


def line_of_four(tokens, cots, sent_cots, cuts, rows, still, scale):
    pairs = [(0, 1), (1, 0), (2, 3), (3, 2)]
    middle = [(1, 2), (2, 1)]
    units, width = rows.shape[1:]
    size = tokens.shape[0]

    def send(block, route):
        return lax.ppermute(block, "tp", route)

    inner_x = send(tokens, middle)
    pair_x = send(tokens, pairs)
    inner_g = send(cots, middle)
    pair_g = send(sent_cots, pairs)
    far_x = send(pair_x, middle)
    *near_terms, top = call(
        inner_forward,
        [array((units, 2 * size), t) for t in (HALF, FULL, FULL)]
        + [array((2, units, width), HALF)],
        (tokens, inner_x, rows),
        after=(still,),
        flops=NEAR_WORK,
        name="near_forward",
    )
    pair_top = send(top, pairs)
    pair_terms = call(
        near_forward,
        [array((units, size), t) for t in (HALF, FULL, FULL)],
        (pair_x, rows),
        after=near_terms[:1],
        flops=PAIR_WORK,
        name="pair_forward",
    )
    pair_part, low = call(
        cut_columns,
        [array((size, cuts[0]), HALF), array((units, width), HALF)],
        (pair_g, rows),
        after=pair_terms[:1],
        name="cut",
    )
    pair_low = send(low, pairs)
    near = call(
        functools.partial(near_backward, scale=scale),
        [array((3, units, width), FULL)],
        (tokens, inner_x, pair_x, cots, inner_g, pair_g, rows, *near_terms, *pair_terms),
        after=(pair_part,),
        name="near_backward",
    )[0]
    *far_terms, pair_more = call(
        far_forward,
        [array((units, size), t) for t in (HALF, FULL, FULL)]
        + [array((size, cuts[1]), HALF)],
        (far_x, rows, pair_g),
        after=(near,),
        name="far_forward",
    )
    far_gs = [send(v, middle) for v in (pair_part, pair_more)]
    hidden, swish, slope = call(
        near_forward,
        [array((units, 2 * size), t) for t in (HALF, FULL, FULL)],
        (inner_x, far_x, pair_top),
        after=(pair_more,),
        flops=AHEAD_WORK,
        name="ahead_forward",
    )
    sizes = [width * v // (7 * 128) * 128 for v in PIECES]
    sizes.append(3 * width - sum(sizes))
    cut, more = sizes[0], sizes[0] + sizes[1] - width
    ends = width - sizes[3]
    first = call(
        functools.partial(pair_first, scale=scale),
        [array((units, sizes[0]), HALF)],
        (inner_x, inner_g, far_gs[0], hidden),
        name="pair_first",
    )[0]
    dgate, dupper = call(
        functools.partial(ahead_backward, scale=scale),
        [array((units, size), HALF)] * 2,
        (inner_g, pair_low, swish, slope),
        after=(first,),
        name="ahead_backward",
    )
    grads = call(
        functools.partial(far_backward, scale=scale),
        [array((3, units, width), FULL)],
        (far_x, *far_gs, rows, *far_terms, near),
        after=(dgate,),
        flops=FAR_WORK,
        name="far_backward",
    )[0]
    second, third, last = call(
        functools.partial(pair_rest, cut=cut, scale=scale),
        [array((units, v), HALF) for v in sizes[1:]],
        (inner_x, far_x, inner_g, *far_gs, pair_low, hidden, swish, slope, dgate, dupper),
        after=(grads,),
        name="pair_rest",
    )
    pieces = [
        ([(2, 0, cut)], first),
        ([(2, cut, width - cut), (1, 0, more)], second),
        ([(1, more, width - more), (0, 0, ends)], third),
        ([(0, ends, sizes[3])], last),
    ]
    pieces = [(tuple(v for v in piece if v[2]), parts) for piece, parts in pieces]
    return grads, pieces, lambda block: send(block, pairs)


def gathered(tokens, cots, rows, scale):
    return unit_grads(
        lax.all_gather(tokens, "tp", axis=0, tiled=True),
        lax.all_gather(cots, "tp", axis=0, tiled=True),
        rows,
        scale,
    )


def still_kernel(rows, first, second, cots, still, step, same_cots):
    master = rows[...].astype(FULL)
    total = adam_step(0.9 * first[...].astype(FULL), 0.95 * second[...].astype(FULL))
    step[...] = total
    still[...] = master - 0.1 * (total + 0.1 * master)

    @pl.when(pl.program_id(0) == 0)
    def _():
        same_cots[...] = cots[...]


def still_values(rows, first, second, cots):
    slab = pl.BlockSpec((1, *rows.shape[1:]), lambda k: (k, 0, 0))
    whole = pl.BlockSpec(cots.shape, lambda k: (0, 0))
    return pl.pallas_call(
        still_kernel,
        grid=(3,),
        out_shape=[array(rows.shape, FULL)] * 2 + [array(cots.shape, cots.dtype)],
        in_specs=[slab] * 3 + [whole],
        out_specs=[slab] * 2 + [whole],
        compiler_params=pltpu.CompilerParams(vmem_limit_bytes=32 * 2**20),
        name="still",
    )(rows, first, second, cots)


def spans(piece):
    start = 0
    for k, first, size in piece:
        yield k, pl.ds(first, size), pl.ds(start, size)
        start += size


def columns_of(piece):
    return sum(size for _, _, size in piece)


def change_kernel(grads, still, still_step, first, second, *rest, piece, parts, ready):
    came, rest = rest[:parts], rest[parts:]
    ready, (updated, sent, *passed) = rest[:ready], rest[ready:]
    for block, same in zip(ready, passed):
        same[...] = block[...]
    for k, place, here in spans(piece):
        grad = grads[k, :, place]
        for part in came:
            grad = grad + part[:, here].astype(FULL)
        moment_one = 0.9 * first[k, :, place].astype(FULL) + 0.1 * grad
        moment_two = 0.95 * second[k, :, place].astype(FULL) + 0.05 * grad * grad
        total = 0.1 * (still_step[k, :, place] - adam_step(moment_one, moment_two))
        updated[:, here] = still[k, :, place] + total
        sent[:, here] = total.astype(HALF)


def change_of(piece, grads, still, still_step, first, second, came, ready, after, flops):
    shape = (grads.shape[1], columns_of(piece))
    return call(
        functools.partial(change_kernel, piece=piece, parts=len(came), ready=len(ready)),
        [array(shape, FULL), array(shape, HALF)] + [array(v.shape, v.dtype) for v in ready],
        (grads, still, still_step, first, second, *came, *ready),
        after=after,
        flops=flops,
        name="change",
    )


def join_kernel(*refs):
    *blocks, joint = refs
    start = 0
    for block in blocks:
        joint[:, pl.ds(start, block.shape[1])] = block[...]
        start += block.shape[1]


def across_kernel(updated, still, far, total, *, piece):
    for k, place, here in spans(piece):
        total[:, here] = updated[:, here] + still[k, :, place] + far[:, here].astype(FULL)


def across_of(i, change, still, after):
    piece, updated, far = change
    return call(
        functools.partial(across_kernel, piece=piece),
        [array(updated.shape, FULL)],
        (updated, still, far),
        after=after,
        flops=ACROSS_WORK[i],
        name="across",
    )[0]


def finish_kernel(*refs, pieces, bands, last):
    parts, near, (total, done) = refs[: len(pieces)], refs[len(pieces)], refs[-2:]
    out = refs[-3 if last else -4]
    if not last:
        refs[-3][...] = jnp.zeros_like(refs[-3])
    units = near.shape[0]
    copies, start = [], 0
    for part, piece in zip(parts, pieces):
        for k, place, here in spans(piece):
            there = pl.ds(start, place.size)
            for i, band in enumerate(bands):
                rows = pl.ds(band, (*bands, units)[i + 1] - band)
                total[rows, there] = (part[rows, here] + near[rows, there]) / 3.0
                copies.append(
                    pltpu.make_async_copy(
                        total.at[rows, there], out.at[k, rows, place], done.at[len(copies)]
                    )
                )
                copies[-1].start()
            start += place.size
    for copy in copies:
        copy.wait()


def finish(pieces, parts, near, shape, held=None):
    units = shape[1]
    bands = (0, units // 32 * 16)
    vmem, anywhere = pl.BlockSpec(memory_space=pltpu.VMEM), pl.BlockSpec(memory_space=pl.ANY)
    held = () if held is None else (held,)
    return pl.pallas_call(
        functools.partial(finish_kernel, pieces=pieces, bands=bands, last=bool(held)),
        out_shape=[array(shape, FULL)] + [array((8, 128), FULL)] * (not held),
        in_specs=[vmem] * (len(parts) + 1) + [anywhere] * len(held),
        out_specs=[anywhere] + [vmem] * (not held),
        input_output_aliases={len(parts) + 1: 0} if held else {},
        scratch_shapes=[
            pltpu.VMEM(near.shape, FULL),
            pltpu.SemaphoreType.DMA((2 * sum(len(v) for v in pieces),)),
        ],
        cost_estimate=pl.CostEstimate(flops=0, bytes_accessed=0, transcendentals=0),
        compiler_params=pltpu.CompilerParams(vmem_limit_bytes=32 * 2**20),
        name="finish",
    )(*parts, near, *held)


def on_device(tokens, cotangent, weights, first_moment, second_moment):
    rows, first, second = (
        jnp.swapaxes(v[0], 0, 1) for v in (weights, first_moment, second_moment)
    )
    scale = (rows.shape[1] * lax.axis_size("tp")) ** (-0.5)
    width = rows.shape[2]
    cuts = (width * PIECES[0] // (7 * 128) * 128,)
    cuts += (width - cuts[0],)
    still, still_step, sent_cots = still_values(rows, first, second, cotangent)
    still_far = neighbour(still, 1)
    if lax.axis_size("tp") == 4:
        grads, pieces, send = line_of_four(
            tokens, cotangent, sent_cots, cuts, rows, still, scale
        )
    else:
        grads = gathered(tokens, cotangent, rows, scale)
        pieces = [([(k, 0, rows.shape[2])], None) for k in ORDER]
    count = len(pieces)
    came = [[] if v is None else [send(v)] for _, v in pieces[:AHEAD]]
    changes, last = [], ()
    for i, (piece, _) in enumerate(pieces):
        ready = [v for _, v in pieces[i + AHEAD : i + AHEAD + 1] if v is not None]
        updated, sent, *ready = change_of(
            piece,
            grads,
            still,
            still_step,
            first,
            second,
            came[i],
            ready,
            last,
            CHANGE_WORK[i],
        )
        came.append([send(v) for v in ready])
        changes.append((piece, updated, neighbour(sent, 1)))
        last = (sent, still_far) if i == STILL_BY else (sent,)
        if i == count - 2:
            totals = [across_of(0, changes[0], still_far, last)]
            last += (totals[0],)
    updates = [v for _, v, _ in changes]
    early = call(
        join_kernel,
        [array((rows.shape[1], 3 * width - updates[-1].shape[1]), FULL)],
        updates[:-1],
        name="join",
    )[0]
    early_near, late_near = neighbour(early, 0), neighbour(updates[-1], 0)
    for i in range(1, count - 1):
        totals.append(across_of(i, changes[i], still_far, (early, totals[-1])))
    places = [v for v, _, _ in changes]
    out, ended = finish(places[:-1], totals, early_near, rows.shape)
    totals.append(across_of(count - 1, changes[-1], still_far, (ended,)))
    (out,) = finish(places[-1:], totals[-1:], late_near, rows.shape, out)
    return jnp.swapaxes(out, 0, 1)[None]


def solution(mesh):
    in_specs = (
        P(("blk", "tp"), None),
        P(("blk", "tp"), None),
        P("blk", "tp", None, None),
        P("blk", "tp", None, None),
        P("blk", "tp", None, None),
    )
    out_specs = P("blk", "tp", None, None)
    return jax.shard_map(
        on_device, mesh=mesh, in_specs=in_specs, out_specs=out_specs, check_vma=False
    )
```

```python
import functools

import jax
import jax.numpy as jnp
from jax import lax
from jax.experimental import pallas as pl
from jax.experimental.pallas import tpu as pltpu
from jax.sharding import PartitionSpec as P

STEP = 10
CORRECT_ONE = 1.0 - 0.9**STEP
CORRECT_TWO = 1.0 - 0.95**STEP
HALF = jnp.bfloat16
FULL = jnp.float32
ORDER = (2, 1, 0)
AHEAD = 2
STILL_BY = 0
PIECES = (5, 5, 6)
NEAR_WORK = 5_000_000_000
PAIR_WORK = 20_000_000_000
AHEAD_WORK = 20_000_000_000
ACROSS_WORK = (20_000_000_000, 2_000_000_000, 60_000_000_000, 30_000_000_000)
FAR_WORK = 0
CHANGE_WORK = (0, 5_000_000_000, 5_000_000_000, 0)


def neighbour(block, side):
    count = lax.axis_size("blk")
    if count % 2:
        route = [((i + 1 - 2 * side) % count, i) for i in range(count)]
    else:
        route = [((side + i) % count, (side + i + 1) % count) for i in range(0, count, 2)]
        route += [(j, i) for i, j in route]
    return lax.ppermute(block, "blk", route)


def adam_step(moment_one, moment_two):
    return moment_one / CORRECT_ONE / (jnp.sqrt(moment_two / CORRECT_TWO) + 1e-08)


def into_units(matrix, values):
    return lax.dot_general(matrix, values, (((1,), (1,)), ((), ())), preferred_element_type=FULL)


def over_tokens(terms, values):
    return lax.dot_general(terms, values, (((1,), (0,)), ((), ())), preferred_element_type=FULL)


def forward_terms(xs, gate_rows, upper_rows):
    scale = xs.shape[1] ** (-0.5)
    gate = into_units(gate_rows, xs) * scale
    upper = into_units(upper_rows, xs) * scale
    sigma = 1.0 / (1.0 + jnp.exp(-gate))
    swish = gate * sigma
    return (swish * upper).astype(HALF), swish, upper * sigma * (1.0 + gate * (1.0 - sigma))


def backward_terms(cots, down_rows, swish, slope, scale):
    back = into_units(down_rows, cots) * scale
    return (back * slope).astype(HALF), (back * swish).astype(HALF)


def unit_grads(xs, cots, rows, scale):
    hidden, swish, slope = forward_terms(xs, rows[0], rows[1])
    dgate, dupper = backward_terms(cots, rows[2], swish, slope, scale)
    width_scale = xs.shape[1] ** (-0.5)
    return jnp.stack(
        [
            over_tokens(dgate, xs) * width_scale,
            over_tokens(dupper, xs) * width_scale,
            over_tokens(hidden, cots) * scale,
        ]
    )


def call(kernel, outs, ins, after=(), flops=0, name=None):
    count = len(ins)

    def body(*refs):
        kernel(*refs[:count], *refs[count + len(after) :])

    return pl.pallas_call(
        body,
        out_shape=outs,
        in_specs=[pl.BlockSpec(memory_space=pltpu.VMEM)] * count
        + [pl.BlockSpec(memory_space=pl.ANY)] * len(after),
        out_specs=[pl.BlockSpec(memory_space=pltpu.VMEM)] * len(outs),
        cost_estimate=pl.CostEstimate(flops=flops, bytes_accessed=0, transcendentals=0),
        compiler_params=pltpu.CompilerParams(vmem_limit_bytes=32 * 2**20),
        name=name,
    )(*ins, *after)


def array(shape, dtype):
    return jax.ShapeDtypeStruct(shape, dtype)


def near_forward(*refs):
    *shards, rows, hidden, swish, slope = refs
    size = shards[0].shape[0]
    for i, xs in enumerate(shards):
        place = pl.ds(i * size, size)
        hidden[:, place], swish[:, place], slope[:, place] = forward_terms(
            xs[...], rows[0], rows[1]
        )


def joined(*parts):
    return jnp.concatenate([v[...] for v in parts], axis=1)


def inner_forward(*refs):
    near_forward(*refs[:-1])
    rows, top = refs[2], refs[-1]
    top[...] = rows[:2]


def near_backward(
    own_x, inner_x, pair_x, own_g, inner_g, pair_g,
    rows, hidden, swish, slope, pair_hidden, pair_swish, pair_slope, grads, *, scale
):
    size, width = own_x.shape
    totals = [0.0, 0.0, 0.0]
    first, second = pl.ds(0, size), pl.ds(size, size)
    shards = (
        (own_x, own_g[...], hidden[:, first], swish[:, first], slope[:, first]),
        (inner_x, inner_g[...], hidden[:, second], swish[:, second], slope[:, second]),
        (pair_x, pair_g[...], pair_hidden[...], pair_swish[...], pair_slope[...]),
    )
    for xs, cots, hid, swi, slo in shards:
        dgate, dupper = backward_terms(cots, rows[2], swi, slo, scale)
        totals[0] += over_tokens(dgate, xs[...])
        totals[1] += over_tokens(dupper, xs[...])
        totals[2] += over_tokens(hid, cots)
    for k in range(3):
        grads[k] = totals[k] * (scale if k == 2 else width ** (-0.5))


def far_forward(far_x, rows, pair_g, hidden, swish, slope, more):
    more[...] = pair_g[:, pair_g.shape[1] - more.shape[1] :]
    hidden[...], swish[...], slope[...] = forward_terms(far_x[...], rows[0], rows[1])


def ahead_backward(inner_g, pair_low, swish, slope, dgate, dupper, *, scale):
    size = inner_g.shape[0]
    dgate[...], dupper[...] = backward_terms(
        inner_g[...], pair_low[...], swish[:, :size], slope[:, :size], scale
    )


def ahead_forward(inner_x, far_x, pair_top, inner_g, hidden, swish, slope, down):
    near_forward(inner_x, far_x, pair_top, hidden, swish, slope)
    size, cut = inner_x.shape[0], down.shape[1]
    down[...] = over_tokens(hidden[:, :size], inner_g[:, :cut])


def pair_first(far_g, hidden, down, sent, *, scale):
    size = far_g.shape[0]
    total = down[...] + over_tokens(hidden[:, size:], far_g[...])
    sent[...] = (total * scale).astype(HALF)


def pair_rest(
    inner_x, far_x, inner_g, far_g, more_g, pair_low, hidden, swish, slope, dgate, dupper,
    second, third, last, *, cut, scale
):
    size, width = inner_x.shape
    width_scale = width ** (-0.5)
    total = over_tokens(hidden[:, :size], inner_g[:, cut:])
    total += over_tokens(hidden[:, size:], more_g[...])
    columns = [(total * scale).astype(HALF)]
    far_terms = backward_terms(
        joined(far_g, more_g), pair_low[...], swish[:, size:], slope[:, size:], scale
    )
    for near, far in zip((dupper, dgate), far_terms[::-1]):
        total = over_tokens(near[...], inner_x[...]) + over_tokens(far, far_x[...])
        columns.append((total * width_scale).astype(HALF))
    columns = jnp.concatenate(columns, axis=1)
    start = 0
    for part in (second, third, last):
        part[...] = columns[:, start : start + part.shape[1]]
        start += part.shape[1]


def far_backward(far_x, far_g, more_g, rows, hidden, swish, slope, near, grads, *, scale):
    width_scale = far_x.shape[1] ** (-0.5)
    cots = joined(far_g, more_g)
    dgate, dupper = backward_terms(cots, rows[2], swish[...], slope[...], scale)
    grads[0] = near[0] + over_tokens(dgate, far_x[...]) * width_scale
    grads[1] = near[1] + over_tokens(dupper, far_x[...]) * width_scale
    grads[2] = near[2] + over_tokens(hidden[...], cots) * scale


def cut_columns(whole, rows, part, low):
    part[...] = whole[:, : part.shape[1]]
    low[...] = rows[2]


def line_of_four(tokens, cots, sent_cots, cuts, rows, still, scale):
    pairs = [(0, 1), (1, 0), (2, 3), (3, 2)]
    middle = [(1, 2), (2, 1)]
    units, width = rows.shape[1:]
    size = tokens.shape[0]

    def send(block, route):
        return lax.ppermute(block, "tp", route)

    inner_x = send(tokens, middle)
    pair_x = send(tokens, pairs)
    inner_g = send(cots, middle)
    pair_g = send(sent_cots, pairs)
    far_x = send(pair_x, middle)
    *near_terms, top = call(
        inner_forward,
        [array((units, 2 * size), t) for t in (HALF, FULL, FULL)]
        + [array((2, units, width), HALF)],
        (tokens, inner_x, rows),
        after=(still,),
        flops=NEAR_WORK,
        name="near_forward",
    )
    pair_top = send(top, pairs)
    pair_terms = call(
        near_forward,
        [array((units, size), t) for t in (HALF, FULL, FULL)],
        (pair_x, rows),
        after=near_terms[:1],
        flops=PAIR_WORK,
        name="pair_forward",
    )
    pair_part, low = call(
        cut_columns,
        [array((size, cuts[0]), HALF), array((units, width), HALF)],
        (pair_g, rows),
        after=pair_terms[:1],
        name="cut",
    )
    pair_low = send(low, pairs)
    near = call(
        functools.partial(near_backward, scale=scale),
        [array((3, units, width), FULL)],
        (tokens, inner_x, pair_x, cots, inner_g, pair_g, rows, *near_terms, *pair_terms),
        after=(pair_part,),
        name="near_backward",
    )[0]
    *far_terms, pair_more = call(
        far_forward,
        [array((units, size), t) for t in (HALF, FULL, FULL)]
        + [array((size, cuts[1]), HALF)],
        (far_x, rows, pair_g),
        after=(near,),
        name="far_forward",
    )
    far_gs = [send(v, middle) for v in (pair_part, pair_more)]
    hidden, swish, slope, down = call(
        ahead_forward,
        [array((units, 2 * size), t) for t in (HALF, FULL, FULL)]
        + [array((units, cuts[0]), FULL)],
        (inner_x, far_x, pair_top, inner_g),
        after=(pair_more,),
        flops=AHEAD_WORK,
        name="ahead_forward",
    )
    sizes = [width * v // (7 * 128) * 128 for v in PIECES]
    sizes.append(3 * width - sum(sizes))
    cut, more = sizes[0], sizes[0] + sizes[1] - width
    ends = width - sizes[3]
    first = call(
        functools.partial(pair_first, scale=scale),
        [array((units, sizes[0]), HALF)],
        (far_gs[0], hidden, down),
        name="pair_first",
    )[0]
    dgate, dupper = call(
        functools.partial(ahead_backward, scale=scale),
        [array((units, size), HALF)] * 2,
        (inner_g, pair_low, swish, slope),
        after=(first,),
        name="ahead_backward",
    )
    grads = call(
        functools.partial(far_backward, scale=scale),
        [array((3, units, width), FULL)],
        (far_x, *far_gs, rows, *far_terms, near),
        after=(dgate,),
        flops=FAR_WORK,
        name="far_backward",
    )[0]
    second, third, last = call(
        functools.partial(pair_rest, cut=cut, scale=scale),
        [array((units, v), HALF) for v in sizes[1:]],
        (inner_x, far_x, inner_g, *far_gs, pair_low, hidden, swish, slope, dgate, dupper),
        after=(grads,),
        name="pair_rest",
    )
    pieces = [
        ([(2, 0, cut)], first),
        ([(2, cut, width - cut), (1, 0, more)], second),
        ([(1, more, width - more), (0, 0, ends)], third),
        ([(0, ends, sizes[3])], last),
    ]
    pieces = [(tuple(v for v in piece if v[2]), parts) for piece, parts in pieces]
    return grads, pieces, lambda block: send(block, pairs)


def gathered(tokens, cots, rows, scale):
    return unit_grads(
        lax.all_gather(tokens, "tp", axis=0, tiled=True),
        lax.all_gather(cots, "tp", axis=0, tiled=True),
        rows,
        scale,
    )


def still_kernel(rows, first, second, cots, still, step, same_cots):
    master = rows[...].astype(FULL)
    total = adam_step(0.9 * first[...].astype(FULL), 0.95 * second[...].astype(FULL))
    step[...] = total
    still[...] = master - 0.1 * (total + 0.1 * master)

    @pl.when(pl.program_id(0) == 0)
    def _():
        same_cots[...] = cots[...]


def still_values(rows, first, second, cots):
    slab = pl.BlockSpec((1, *rows.shape[1:]), lambda k: (k, 0, 0))
    whole = pl.BlockSpec(cots.shape, lambda k: (0, 0))
    return pl.pallas_call(
        still_kernel,
        grid=(3,),
        out_shape=[array(rows.shape, FULL)] * 2 + [array(cots.shape, cots.dtype)],
        in_specs=[slab] * 3 + [whole],
        out_specs=[slab] * 2 + [whole],
        compiler_params=pltpu.CompilerParams(vmem_limit_bytes=32 * 2**20),
        name="still",
    )(rows, first, second, cots)


def spans(piece):
    start = 0
    for k, first, size in piece:
        yield k, pl.ds(first, size), pl.ds(start, size)
        start += size


def columns_of(piece):
    return sum(size for _, _, size in piece)


def change_kernel(grads, still, still_step, first, second, *rest, piece, parts, ready):
    came, rest = rest[:parts], rest[parts:]
    ready, (updated, sent, *passed) = rest[:ready], rest[ready:]
    for block, same in zip(ready, passed):
        same[...] = block[...]
    for k, place, here in spans(piece):
        grad = grads[k, :, place]
        for part in came:
            grad = grad + part[:, here].astype(FULL)
        moment_one = 0.9 * first[k, :, place].astype(FULL) + 0.1 * grad
        moment_two = 0.95 * second[k, :, place].astype(FULL) + 0.05 * grad * grad
        total = 0.1 * (still_step[k, :, place] - adam_step(moment_one, moment_two))
        updated[:, here] = still[k, :, place] + total
        sent[:, here] = total.astype(HALF)


def change_of(piece, grads, still, still_step, first, second, came, ready, after, flops):
    shape = (grads.shape[1], columns_of(piece))
    return call(
        functools.partial(change_kernel, piece=piece, parts=len(came), ready=len(ready)),
        [array(shape, FULL), array(shape, HALF)] + [array(v.shape, v.dtype) for v in ready],
        (grads, still, still_step, first, second, *came, *ready),
        after=after,
        flops=flops,
        name="change",
    )


def join_kernel(*refs):
    *blocks, joint = refs
    start = 0
    for block in blocks:
        joint[:, pl.ds(start, block.shape[1])] = block[...]
        start += block.shape[1]


def across_kernel(updated, still, far, total, *, piece):
    for k, place, here in spans(piece):
        total[:, here] = updated[:, here] + still[k, :, place] + far[:, here].astype(FULL)


def across_of(i, change, still, after):
    piece, updated, far = change
    return call(
        functools.partial(across_kernel, piece=piece),
        [array(updated.shape, FULL)],
        (updated, still, far),
        after=after,
        flops=ACROSS_WORK[i],
        name="across",
    )[0]


def finish_kernel(*refs, pieces, bands, last):
    parts, near, (total, done) = refs[: len(pieces)], refs[len(pieces)], refs[-2:]
    out = refs[-3 if last else -4]
    if not last:
        refs[-3][...] = jnp.zeros_like(refs[-3])
    units = near.shape[0]
    copies, start = [], 0
    for part, piece in zip(parts, pieces):
        for k, place, here in spans(piece):
            there = pl.ds(start, place.size)
            for i, band in enumerate(bands):
                rows = pl.ds(band, (*bands, units)[i + 1] - band)
                total[rows, there] = (part[rows, here] + near[rows, there]) / 3.0
                copies.append(
                    pltpu.make_async_copy(
                        total.at[rows, there], out.at[k, rows, place], done.at[len(copies)]
                    )
                )
                copies[-1].start()
            start += place.size
    for copy in copies:
        copy.wait()


def finish(pieces, parts, near, shape, held=None):
    units = shape[1]
    bands = (0, units // 32 * 16)
    vmem, anywhere = pl.BlockSpec(memory_space=pltpu.VMEM), pl.BlockSpec(memory_space=pl.ANY)
    held = () if held is None else (held,)
    return pl.pallas_call(
        functools.partial(finish_kernel, pieces=pieces, bands=bands, last=bool(held)),
        out_shape=[array(shape, FULL)] + [array((8, 128), FULL)] * (not held),
        in_specs=[vmem] * (len(parts) + 1) + [anywhere] * len(held),
        out_specs=[anywhere] + [vmem] * (not held),
        input_output_aliases={len(parts) + 1: 0} if held else {},
        scratch_shapes=[
            pltpu.VMEM(near.shape, FULL),
            pltpu.SemaphoreType.DMA((2 * sum(len(v) for v in pieces),)),
        ],
        cost_estimate=pl.CostEstimate(flops=0, bytes_accessed=0, transcendentals=0),
        compiler_params=pltpu.CompilerParams(vmem_limit_bytes=32 * 2**20),
        name="finish",
    )(*parts, near, *held)


def on_device(tokens, cotangent, weights, first_moment, second_moment):
    rows, first, second = (
        jnp.swapaxes(v[0], 0, 1) for v in (weights, first_moment, second_moment)
    )
    scale = (rows.shape[1] * lax.axis_size("tp")) ** (-0.5)
    width = rows.shape[2]
    cuts = (width * PIECES[0] // (7 * 128) * 128,)
    cuts += (width - cuts[0],)
    still, still_step, sent_cots = still_values(rows, first, second, cotangent)
    still_far = neighbour(still, 1)
    if lax.axis_size("tp") == 4:
        grads, pieces, send = line_of_four(
            tokens, cotangent, sent_cots, cuts, rows, still, scale
        )
    else:
        grads = gathered(tokens, cotangent, rows, scale)
        pieces = [([(k, 0, rows.shape[2])], None) for k in ORDER]
    count = len(pieces)
    came = [[] if v is None else [send(v)] for _, v in pieces[:AHEAD]]
    changes, last = [], ()
    for i, (piece, _) in enumerate(pieces):
        ready = [v for _, v in pieces[i + AHEAD : i + AHEAD + 1] if v is not None]
        updated, sent, *ready = change_of(
            piece,
            grads,
            still,
            still_step,
            first,
            second,
            came[i],
            ready,
            last,
            CHANGE_WORK[i],
        )
        came.append([send(v) for v in ready])
        changes.append((piece, updated, neighbour(sent, 1)))
        last = (sent, still_far) if i == STILL_BY else (sent,)
        if i == count - 2:
            totals = [across_of(0, changes[0], still_far, last)]
            last += (totals[0],)
    updates = [v for _, v, _ in changes]
    early = call(
        join_kernel,
        [array((rows.shape[1], 3 * width - updates[-1].shape[1]), FULL)],
        updates[:-1],
        name="join",
    )[0]
    early_near, late_near = neighbour(early, 0), neighbour(updates[-1], 0)
    for i in range(1, count - 1):
        totals.append(across_of(i, changes[i], still_far, (early, totals[-1])))
    places = [v for v, _, _ in changes]
    out, ended = finish(places[:-1], totals, early_near, rows.shape)
    totals.append(across_of(count - 1, changes[-1], still_far, (ended,)))
    (out,) = finish(places[-1:], totals[-1:], late_near, rows.shape, out)
    return jnp.swapaxes(out, 0, 1)[None]


def solution(mesh):
    in_specs = (
        P(("blk", "tp"), None),
        P(("blk", "tp"), None),
        P("blk", "tp", None, None),
        P("blk", "tp", None, None),
        P("blk", "tp", None, None),
    )
    out_specs = P("blk", "tp", None, None)
    return jax.shard_map(
        on_device, mesh=mesh, in_specs=in_specs, out_specs=out_specs, check_vma=False
    )
```
